256 devices in a mesh: dp: 8 (over y, core), expert: 32 (over z, x).
Axes of the slice: x: 4, y: 4, z: 8, core: 2. Of those that a mesh axis runs over, the one named last changes fastest.
Arguments:
- frames: bfloat16 [49152, 1024], P(('dp', 'expert')), may hold values from -6 to 6
- norm_gain_vector: float32 [1024], replicated, may hold values from 0.1 to 1.9
- router: bfloat16 [1024, 32], replicated, may hold values from -0.1875 to 0.1875
- w_in: bfloat16 [32, 1024, 2048], P('expert', 'dp'), may hold values from -0.1875 to 0.1875
- w_out: bfloat16 [32, 2048, 1024], P('expert', 'dp'), may hold values from -0.125 to 0.125
- expert_ids: int32 [49152, 2], P(('dp', 'expert')), may hold values from 0 to 31, all different within a row; in each aligned block of 192 rows (0 to 191, 192 to 383, ...) at most 18 rows name the same one
- frame_mask: int32 [49152], P(('dp', 'expert')), may hold values 0 or 1
- out_grad: bfloat16 [49152, 1024], P(('dp', 'expert')), may hold values from -6 to 6
Outputs:
- mixed: bfloat16 [49152, 1024], P(('dp', 'expert'))
- grad_frames: bfloat16 [49152, 1024], P(('dp', 'expert'))
- grad_w_in: float32 [32, 1024, 2048], P('expert', 'dp')
- grad_w_out: float32 [32, 2048, 1024], P('expert', 'dp')
- grad_router: float32 [1024, 32], replicated
- gain_gradient: float32 [1024], replicated
The draws below stay inside these ranges and needn't reach their ends.
Inputs may be any that keep to these rules, and one draw needn't show every extreme that they name: `expert_ids`: each row names two different experts; among the frames of one device no expert is named more than 18 times, a bound that some block reaches.
All inputs are finite; a program needn't handle non-finite values. No bound on the sum of `frame_mask` on one device may be relied on, other than what follows from the above.
Results may differ from the reference program's by a relative error of at most 0.015.
Values may be sent and summed in bfloat16 or wider, within the bound.
No kernel may reach another device: no remote copies, remote signals or barrier semaphores. Data moves between devices by JAX's collectives and lax.ppermute only.
A program may use at most 128 MiB of HBM per device.

```python
import math
import jax
import jax.numpy as jnp
import numpy as np
from jax import lax

D = 1024
FF = 2048
EXPERTS = 32
TOPK = 2
FR_DEV = 192
CAP = 18
FRAMES = 49152
N_DP = 8
N_EXPERT = 32


def touch_ends(values, stream_key, smallest, high):
    shape = values.shape
    spot = [jax.random.randint(jax.random.fold_in(stream_key, axis), (), 0, shape[axis]) for axis in range(len(shape))]
    values = values.at[tuple(spot)].set(smallest)
    longest = shape.index(max(shape))
    spot[longest] = (spot[longest] + 1) % shape[longest]
    return values.at[tuple(spot)].set(high)


def levels(rng, extent, pieces, smallest, largest):
    loudness = 1.0
    for dim, blocks in pieces:
        draws = jax.random.uniform(jax.random.fold_in(jax.random.fold_in(rng, 6), dim), (blocks,), jnp.float32, smallest / len(pieces), largest / len(pieces))
        loudness = loudness * jnp.repeat(jnp.exp(draws), extent[dim] // blocks).reshape((-1,) + (1,) * (len(extent) - 1 - dim))
    return loudness


def routed_block(stream_key, own, number, rows, number_of, top, bound, skew):
    order = jax.random.permutation(stream_key, number_of)
    packed, usual = portions_of(number_of, rows * top, bound, skew, True), portions_of(number_of, rows * top, bound, skew, False)
    places = jnp.arange(number_of)

    def named(lengths, rotation):
        used = int((lengths > 0).sum())
        fixed = max(1, used // 4)
        moved = fixed + (places - fixed + rotation * (used - fixed)) % max(1, number_of - fixed)
        return jnp.zeros((number_of,), jnp.int32).at[order[jnp.where(places < fixed, places, moved)]].set(jnp.asarray(lengths, jnp.int32))

    lengths = jnp.where(number % 4 == 0, named(packed, number // 4), named(usual, number - number // 4 - 1))
    mixed = jax.random.permutation(jax.random.fold_in(own, 3), number_of)
    giver, receiver = mixed[0:number_of // 2 * 2:2], mixed[1:number_of // 2 * 2:2]
    margin = jnp.minimum(lengths[giver] - 1, bound - lengths[receiver]) // 2
    margin = jnp.where((giver == order[0]) | (receiver == order[0]) | (lengths[receiver] == 0), 0, jnp.maximum(margin, 0))
    moved = jax.random.randint(jax.random.fold_in(own, 4), (number_of // 2,), 0, 1 << 20) % (margin + 1)
    lengths = lengths.at[giver].add(-moved).at[receiver].add(moved)
    items = jnp.searchsorted(jnp.cumsum(lengths), jnp.arange(rows * top), side="right").astype(jnp.int32)
    listing = items.reshape(top, rows).T
    listing = listing[jax.random.permutation(jax.random.fold_in(own, 1), rows)]
    rotation = jax.random.randint(jax.random.fold_in(own, 2), (rows, 1), 0, top)
    return jnp.take_along_axis(listing, (jnp.arange(top)[None, :] + rotation) % top, axis=1)


def portions_of(amount, total, limit, slope, full):
    portions = [(1 << 20) // math.isqrt(standing ** slope) + 1 for standing in range(1, amount + 1)]
    largest = limit if full else min(limit, max(-(-total // amount), total * portions[0] // sum(portions)))
    least = 1 if total - largest >= amount - 1 else 0
    holding, rest = [largest] + [least] * (amount - 1), total - largest - least * (amount - 1)
    while rest > 0:
        movable = [i for i in range(1, amount) if holding[i] < largest] or [i for i in range(1, amount) if holding[i] < limit]
        mass, left = sum([portions[i] for i in movable]), rest
        for i in movable:
            addition = min(limit - holding[i], max(1, left * portions[i] // mass), rest)
            holding[i] = holding[i] + addition
            rest = rest - addition
    return np.array(holding)


def normal_values(stream_key, extent, deviation, limit, split=(), held_as=jnp.bfloat16):
    entries = jax.random.normal(stream_key, extent, jnp.float32) * deviation
    if len(split) > 0:
        entries = levels(stream_key, extent, split, -0.22, 0.18) * entries
    return jnp.clip(entries, min=-limit, max=limit).astype(held_as)


def setup_inputs(seed: int = 0) -> dict:
    splits = jax.random.split(jax.random.key(seed), 9)
    frames = normal_values(splits[0], (FRAMES, D), 1.0, 6.0, ((0, 256),))
    norm_gain_vector = jnp.clip(1.0 + 0.18 * jax.random.normal(splits[1], (D,), jnp.float32), 0.1, 1.9)
    router = normal_values(splits[2], (D, EXPERTS), D ** -0.5, 0.1875)
    w_in = normal_values(splits[3], (EXPERTS, D, FF), D ** -0.5, 0.1875, ((0, 32), (1, 8)))
    w_out = normal_values(splits[4], (EXPERTS, FF, D), FF ** -0.5, 0.125, ((0, 32), (1, 8)))
    expert_ids_keys = jax.random.split(jax.random.fold_in(splits[5], 1), FRAMES // FR_DEV)
    expert_ids_turns = jax.random.permutation(jax.random.fold_in(splits[5], 3), FRAMES // FR_DEV)
    expert_ids = jax.vmap(lambda own, number: routed_block(jax.random.fold_in(splits[5], 2), own, number, FR_DEV, EXPERTS, TOPK, CAP, 2))(expert_ids_keys, expert_ids_turns).reshape((FRAMES, TOPK))
    frame_mask = touch_ends((jax.random.randint(splits[6], (FRAMES,), 0, 4) < 3).astype(jnp.int32), jax.random.fold_in(splits[6], 1), 0, 1)
    out_grad = normal_values(splits[7], (FRAMES, D), 1.0, 6.0, ((0, 256),))
    return dict(frames=frames, norm_gain_vector=norm_gain_vector, router=router, w_in=w_in, w_out=w_out, expert_ids=expert_ids, frame_mask=frame_mask, out_grad=out_grad)


EPS = 1e-05

def slots_of(flat_ids):
    onehot = (flat_ids[..., None] == jnp.arange(EXPERTS, dtype=jnp.int32)).astype(jnp.int32)
    before = jnp.cumsum(onehot, axis=1) - onehot
    return lax.optimization_barrier(jnp.sum(before * onehot, axis=2)).astype(jnp.int32)

def reference(frames, norm_gain_vector, router, w_in, w_out, expert_ids, frame_mask, out_grad):
    devices = N_DP * N_EXPERT
    floats = frames.astype(jnp.float32)
    average = lax.optimization_barrier(jnp.mean(floats, axis=1, keepdims=True))
    centered_input = floats - average
    inverse_deviation = lax.rsqrt(lax.optimization_barrier(jnp.mean(centered_input * centered_input, axis=1, keepdims=True)) + EPS)
    standardized_input = centered_input * inverse_deviation
    normalized_rows = (standardized_input * norm_gain_vector).astype(jnp.bfloat16)
    logits = jnp.dot(normalized_rows, router, preferred_element_type=jnp.float32)
    choose = (expert_ids[:, :, None] == jnp.arange(EXPERTS, dtype=jnp.int32)[None, None, :]).astype(jnp.float32)
    picked_logit = lax.optimization_barrier(jnp.sum(logits[:, None, :] * choose, axis=2))
    scores = jax.nn.sigmoid(picked_logit)
    totals = lax.optimization_barrier(jnp.sum(scores, axis=1, keepdims=True))
    live_mask = frame_mask.astype(jnp.float32)[:, None]
    weight = live_mask * scores / totals
    slot_pair = slots_of(expert_ids.reshape(devices, FR_DEV * TOPK)).reshape(FRAMES, TOPK)
    source = jnp.broadcast_to((jnp.arange(FRAMES, dtype=jnp.int32) // FR_DEV)[:, None], (FRAMES, TOPK))
    spread_rows = jnp.broadcast_to(normalized_rows[:, None, :], (FRAMES, TOPK, D))
    buffer = jnp.zeros((EXPERTS, devices, CAP, D), jnp.bfloat16).at[expert_ids, source, slot_pair].set(spread_rows)

    def forward_one(inputs):
        expert_rows, matrix_in, matrix_out = inputs
        flat_rows = expert_rows.reshape(devices * CAP, D)
        pre_act = jnp.dot(flat_rows, matrix_in, preferred_element_type=jnp.float32)
        hidden = (pre_act * jax.nn.sigmoid(pre_act)).astype(jnp.bfloat16)
        result = jnp.dot(hidden, matrix_out, preferred_element_type=jnp.float32).astype(jnp.bfloat16)
        return result.reshape(devices, CAP, D)
    expert_out = lax.map(forward_one, (buffer, w_in, w_out))
    picked = expert_out[expert_ids, source, slot_pair]
    mixed = (floats + lax.optimization_barrier(jnp.sum(weight[:, :, None] * picked.astype(jnp.float32), axis=1))).astype(jnp.bfloat16)
    grad_f = out_grad.astype(jnp.float32)
    grad_weight = lax.optimization_barrier(jnp.sum(grad_f[:, None, :] * picked.astype(jnp.float32), axis=2))
    grad_rows_in = (weight[:, :, None] * grad_f[:, None, :]).astype(jnp.bfloat16)
    grad_buffer = jnp.zeros((EXPERTS, devices, CAP, D), jnp.bfloat16).at[expert_ids, source, slot_pair].set(grad_rows_in)

    def backward_one(inputs):
        expert_rows, expert_grads, matrix_in, matrix_out = inputs
        flat_rows = expert_rows.reshape(devices * CAP, D)
        flat_grads = expert_grads.reshape(devices * CAP, D)
        pre_act = jnp.dot(flat_rows, matrix_in, preferred_element_type=jnp.float32)
        logistic = jax.nn.sigmoid(pre_act)
        hidden = (pre_act * logistic).astype(jnp.bfloat16)
        derivative = logistic * (1.0 + pre_act * (1.0 - logistic))
        grad_hidden = jnp.dot(flat_grads, matrix_out.T, preferred_element_type=jnp.float32)
        grad_pre = (grad_hidden * derivative).astype(jnp.bfloat16)
        grad_rows = jnp.dot(grad_pre, matrix_in.T, preferred_element_type=jnp.float32).astype(jnp.bfloat16)
        group_rows = flat_rows.reshape(N_DP, N_EXPERT * CAP, D).astype(jnp.float32)
        group_pre = grad_pre.reshape(N_DP, N_EXPERT * CAP, FF).astype(jnp.float32)
        group_hidden = hidden.reshape(N_DP, N_EXPERT * CAP, FF).astype(jnp.float32)
        group_grads = flat_grads.reshape(N_DP, N_EXPERT * CAP, D).astype(jnp.float32)
        part_in = jnp.einsum('grd,grf->gdf', group_rows, group_pre, precision=lax.Precision.HIGHEST)
        part_out = jnp.einsum('grf,grd->gfd', group_hidden, group_grads, precision=lax.Precision.HIGHEST)
        part_in = lax.optimization_barrier(part_in.astype(jnp.bfloat16)).astype(jnp.float32)
        part_out = lax.optimization_barrier(part_out.astype(jnp.bfloat16)).astype(jnp.float32)
        return (grad_rows.reshape(devices, CAP, D), lax.optimization_barrier(jnp.sum(part_in, axis=0)), lax.optimization_barrier(jnp.sum(part_out, axis=0)))
    grad_back, grad_w_in, grad_w_out = lax.map(backward_one, (buffer, grad_buffer, w_in, w_out))
    grad_moe = lax.optimization_barrier(jnp.sum(grad_back[expert_ids, source, slot_pair].astype(jnp.float32), axis=1))
    first_score = scores[:, 0]
    second_score = scores[:, 1]
    sum_scores = totals[:, 0]
    weight_gap = grad_weight[:, 0] - grad_weight[:, 1]
    live_flat = live_mask[:, 0]
    grad_first = live_flat * weight_gap * second_score / (sum_scores * sum_scores)
    grad_second = -live_flat * weight_gap * first_score / (sum_scores * sum_scores)
    grad_picked = jnp.stack([grad_first, grad_second], axis=1) * scores * (1.0 - scores)
    grad_logits = lax.optimization_barrier(jnp.sum(grad_picked[:, :, None] * choose, axis=1))
    normalized_gradient = grad_moe + jnp.dot(grad_logits, router.astype(jnp.float32).T, precision=lax.Precision.HIGHEST)
    grad_router = jnp.dot(normalized_rows.astype(jnp.float32).T, grad_logits, precision=lax.Precision.HIGHEST)
    gain_gradient = lax.optimization_barrier(jnp.sum(normalized_gradient * standardized_input, axis=0))
    standardized_gradient = normalized_gradient * norm_gain_vector
    statistic_gradient = inverse_deviation * (standardized_gradient - lax.optimization_barrier(jnp.mean(standardized_gradient, axis=1, keepdims=True)) - standardized_input * lax.optimization_barrier(jnp.mean(standardized_gradient * standardized_input, axis=1, keepdims=True)))
    grad_frames = (grad_f + statistic_gradient).astype(jnp.bfloat16)
    return (mixed, grad_frames, grad_w_in, grad_w_out, grad_router, gain_gradient)
```

```python
import functools

import jax
import jax.numpy as jnp
from jax import lax
from jax.experimental import pallas as pl
from jax.experimental.pallas import tpu as pltpu
from jax.sharding import PartitionSpec as P

CAP = 18
MAIN = 16
EPS = 1e-05
LANES = 128

f32 = jnp.float32
bf16 = jnp.bfloat16


def iota(shape, dim):
    return lax.broadcasted_iota(jnp.int32, shape, dim)


def indicator(condition):
    return jnp.where(condition, 1.0, 0.0).astype(bf16)


def matmul(a, b, **kw):
    return jnp.dot(a, b, preferred_element_type=f32, **kw)


def matmul_nt(a, b, **kw):
    return lax.dot_general(a, b, (((1,), (1,)), ((), ())), preferred_element_type=f32, **kw)


def extra_order(peers, pieces):
    rows = peers * MAIN
    i = iota((rows, rows), 0)
    j = iota((rows, rows), 1)
    return i, j, rows


def pack(rows, out_ref, peers):
    width = rows.shape[1]
    pieces = width // LANES
    main = peers * MAIN
    out_ref[:, :width] = rows[:main]
    extra = rows[main:]
    stacked = jnp.concatenate([extra[:, p * LANES : (p + 1) * LANES] for p in range(pieces)], axis=0)
    i, j, _ = extra_order(peers, pieces)
    source = (i % pieces) * (2 * peers) + ((i // pieces) % 2) * peers + i // MAIN
    out_ref[:, width:] = matmul(indicator(j == source), stacked).astype(bf16)


def unpack(ref, peers):
    width = ref.shape[1] - LANES
    pieces = width // LANES
    i, j, _ = extra_order(peers, pieces)
    target = (i % peers) * MAIN + ((i // peers) % 2) * pieces + i // (2 * peers)
    stacked = matmul(indicator(j == target), ref[:, width:]).astype(bf16)
    extra = jnp.concatenate(
        [stacked[p * 2 * peers : (p + 1) * 2 * peers] for p in range(pieces)], axis=1
    )
    return ref[:, :width], extra


def layer_norm(frames_ref):
    floats = frames_ref[...].astype(f32)
    average = jnp.mean(floats, axis=1, keepdims=True)
    centered = floats - average
    inverse = lax.rsqrt(jnp.mean(centered * centered, axis=1, keepdims=True) + EPS)
    return floats, centered * inverse, inverse


def dispatch_kernel(peers, frames_ref, gain_ref, ids_ref, out_ref, normed_ref, place_ref):
    _, standardized, _ = layer_norm(frames_ref)
    normed = (standardized * gain_ref[...]).astype(bf16)
    normed_ref[...] = normed
    count = normed.shape[0]
    ids = ids_ref[...]
    expert = iota((peers, count), 0)
    first, second = expert == ids[0:1], expert == ids[1:2]
    earlier = indicator(iota((count, count), 0) < iota((count, count), 1))
    before = matmul(indicator(first | second), earlier)
    places = []
    for k, chosen in enumerate((first, second)):
        slot = jnp.sum(jnp.where(chosen, before, 0.0), axis=0, keepdims=True).astype(jnp.int32)
        e = ids[k : k + 1]
        places.append(
            jnp.where(slot < MAIN, e * MAIN + slot, peers * MAIN + (slot - MAIN) * peers + e)
        )
    place = jnp.concatenate(places, axis=0)
    place_ref[...] = place
    row = iota((peers * CAP, count), 0)
    select = indicator((row == place[0:1]) | (row == place[1:2]))
    pack(matmul(select, normed).astype(bf16), out_ref, peers)


def grads_kernel(peers, normed_ref, router_ref, ids_ref, mask_ref, place_ref, grad_ref, out_ref, meta_ref):
    logits = matmul_nt(router_ref[...], normed_ref[...])
    count = logits.shape[1]
    ids = ids_ref[...]
    place = place_ref[...]
    expert = iota((peers, count), 0)
    scores = [
        jax.nn.sigmoid(
            jnp.sum(jnp.where(expert == ids[k : k + 1], logits, 0.0), axis=0, keepdims=True)
        )
        for k in range(2)
    ]
    total = scores[0] + scores[1]
    live = mask_ref[...].astype(f32)
    weights = [live * s / total for s in scores]
    row = iota((peers * CAP, count), 0)
    here = [row == place[k : k + 1] for k in range(2)]
    scale = jnp.sum(
        jnp.where(here[0], weights[0], 0.0) + jnp.where(here[1], weights[1], 0.0),
        axis=1,
        keepdims=True,
    )
    rows = matmul(indicator(here[0] | here[1]), grad_ref[...])
    pack((rows * scale).astype(bf16), out_ref, peers)
    facts = jnp.concatenate(
        [
            place.astype(f32),
            ids.astype(f32),
            weights[0],
            weights[1],
            scores[0],
            scores[1],
        ],
        axis=0,
    )
    padded = jnp.concatenate([facts, jnp.zeros((8, 256 - count), f32)], axis=1)
    meta_ref[...] = padded.T[:count]


def unpack_kernel(peers, packed_ref, out_ref):
    main, extra = unpack(packed_ref, peers)
    out_ref[: peers * MAIN] = main
    out_ref[peers * MAIN :] = extra


def pack_kernel(peers, rows_ref, out_ref):
    pack(rows_ref[...], out_ref, peers)


def mix_kernel(
    peers, packed_ref, frames_ref, normed_ref, grad_ref, meta_ref, mask_ref, router_ref,
    mixed_ref, base_ref, router_part_ref,
):
    main, extra = unpack(packed_ref, peers)
    meta = meta_ref[...]
    column = [meta[:, k : k + 1] for k in range(8)]
    count = meta.shape[0]
    places = [c.astype(jnp.int32) for c in column[0:2]]
    experts = [c.astype(jnp.int32) for c in column[2:4]]
    weights, scores = column[4:6], column[6:8]
    cut = peers * MAIN
    lane = iota((count, cut), 1)
    lane_extra = iota((count, 2 * peers), 1) + cut
    grad = grad_ref[...].astype(f32)
    picked = [
        matmul(indicator(lane == p), main) + matmul(indicator(lane_extra == p), extra)
        for p in places
    ]
    mixed = frames_ref[...].astype(f32) + (weights[0] * picked[0] + weights[1] * picked[1])
    mixed_ref[...] = mixed.astype(bf16)
    grad_weight = [jnp.sum(grad * p, axis=1, keepdims=True) for p in picked]
    total = scores[0] + scores[1]
    gap = mask_ref[...].astype(f32) * (grad_weight[0] - grad_weight[1]) / (total * total)
    first = gap * scores[1] * scores[0] * (1.0 - scores[0])
    second = -gap * scores[0] * scores[1] * (1.0 - scores[1])
    which = iota((count, peers), 1)
    grad_logits = jnp.where(which == experts[0], first, 0.0) + jnp.where(
        which == experts[1], second, 0.0
    )
    base_ref[...] = matmul(grad_logits, router_ref[...].astype(f32), precision=lax.Precision.HIGHEST)
    router_part_ref[...] = lax.dot_general(
        grad_logits,
        normed_ref[...].astype(f32),
        (((0,), (0,)), ((), ())),
        precision=lax.Precision.HIGHEST,
        preferred_element_type=f32,
    )


def finish_kernel(
    peers, packed_ref, frames_ref, gain_ref, grad_ref, meta_ref, base_ref, out_ref, gain_part_ref
):
    main, extra = unpack(packed_ref, peers)
    meta = meta_ref[...]
    count = meta.shape[0]
    places = [meta[:, k : k + 1].astype(jnp.int32) for k in range(2)]
    cut = peers * MAIN
    lane = iota((count, cut), 1)
    lane_extra = iota((count, 2 * peers), 1) + cut
    grad_moe = matmul(indicator((lane == places[0]) | (lane == places[1])), main) + matmul(
        indicator((lane_extra == places[0]) | (lane_extra == places[1])), extra
    )
    _, standardized, inverse = layer_norm(frames_ref)
    grad_normed = grad_moe + base_ref[...]
    gain_part_ref[...] = jnp.sum(grad_normed * standardized, axis=0, keepdims=True)
    g = grad_normed * gain_ref[...]
    statistic = inverse * (
        g
        - jnp.mean(g, axis=1, keepdims=True)
        - standardized * jnp.mean(g * standardized, axis=1, keepdims=True)
    )
    out_ref[...] = (grad_ref[...].astype(f32) + statistic).astype(bf16)


def call(kernel, name, *outs, flops=0):
    params = pltpu.CompilerParams(vmem_limit_bytes=48 * 1024 * 1024)

    def run(*args):
        size = sum(a.size * a.dtype.itemsize for a in args)
        size += sum(o.size * o.dtype.itemsize for o in outs)
        return pl.pallas_call(
            kernel,
            out_shape=outs if len(outs) > 1 else outs[0],
            compiler_params=params,
            cost_estimate=pl.CostEstimate(flops=flops, bytes_accessed=size, transcendentals=0),
            name=name,
        )(*args)

    return run


def shape(*dims, dtype=bf16):
    return jax.ShapeDtypeStruct(dims, dtype)


def exchange(packed, peers):
    out = lax.all_to_all(
        packed.reshape(peers, MAIN, packed.shape[1]), "expert", split_axis=0, concat_axis=0, tiled=True
    )
    return out.reshape(packed.shape)


def sum_over_all(rows, peers, groups):
    width = rows.shape[1]
    blocks = rows.reshape(peers, 8, width // 8)
    mine = jnp.sum(lax.all_to_all(blocks, "expert", 0, 0, tiled=True), axis=0)
    spread = jnp.broadcast_to(mine[None], (groups,) + mine.shape)
    mine = jnp.sum(lax.all_to_all(spread, "dp", 0, 0, tiled=True), axis=0)
    spread = jnp.broadcast_to(mine[None], (peers,) + mine.shape)
    return lax.all_to_all(spread, "expert", 0, 0, tiled=True).reshape(rows.shape)


def on_device(groups, frames, gain, router, w_in, w_out, expert_ids, frame_mask, out_grad):
    count, width = frames.shape
    peers = router.shape[1]
    rows = peers * CAP
    packed = shape(peers * MAIN, width + LANES)
    gain = gain[None]
    router_rows = router.T
    ids = expert_ids.T
    weights_in = lax.all_gather(w_in[0], "dp", axis=0, tiled=True)
    weights_out = lax.all_gather(w_out[0], "dp", axis=0, tiled=True)

    part = functools.partial
    sent, normed, place = call(
        part(dispatch_kernel, peers), "dispatch", packed, shape(count, width), shape(2, count, dtype=jnp.int32)
    )(frames, gain, ids)
    arrived = exchange(sent, peers)
    sent_grads, meta = call(
        part(grads_kernel, peers), "grads", packed, shape(count, 8, dtype=f32)
    )(normed, router_rows, ids, frame_mask[None], place, out_grad)
    arrived_grads = exchange(sent_grads, peers)

    incoming = call(part(unpack_kernel, peers), "unpack", shape(rows, width))(arrived)
    pre = matmul(incoming, weights_in)
    logistic = jax.nn.sigmoid(pre)
    hidden = (pre * logistic).astype(bf16)
    derivative = logistic * (1.0 + pre * (1.0 - logistic))
    expert_out = matmul(hidden, weights_out).astype(bf16)
    returned = exchange(call(part(pack_kernel, peers), "pack", packed)(expert_out), peers)

    grad_incoming = call(part(unpack_kernel, peers), "unpack_grads", shape(rows, width))(arrived_grads)
    part_out = lax.dot_general(
        hidden, grad_incoming, (((0,), (0,)), ((), ())), preferred_element_type=f32
    ).astype(bf16)
    grad_w_out = lax.psum_scatter(part_out, "dp", scatter_dimension=0, tiled=True).astype(f32)
    grad_pre = (matmul_nt(grad_incoming, weights_out) * derivative).astype(bf16)
    part_in = lax.dot_general(
        incoming, grad_pre, (((0,), (0,)), ((), ())), preferred_element_type=f32
    ).astype(bf16)
    grad_w_in = lax.psum_scatter(part_in, "dp", scatter_dimension=0, tiled=True).astype(f32)
    grad_rows = matmul_nt(grad_pre, weights_in).astype(bf16)
    back = exchange(call(part(pack_kernel, peers), "pack_grads", packed)(grad_rows), peers)

    mixed, base, router_part = call(
        part(mix_kernel, peers),
        "mix",
        shape(count, width),
        shape(count, width, dtype=f32),
        shape(peers, width, dtype=f32),
    )(returned, frames, normed, out_grad, meta, frame_mask[:, None], router_rows)
    grad_router = sum_over_all(router_part, peers, groups).T
    grad_frames, gain_part = call(
        part(finish_kernel, peers), "finish", shape(count, width), shape(1, width, dtype=f32)
    )(back, frames, gain, out_grad, meta, base)
    spread = jnp.broadcast_to(gain_part.reshape(1, 8, width // 8), (peers, 8, width // 8))
    gain_mine = jnp.sum(lax.all_to_all(spread, "expert", 0, 0, tiled=True), axis=0)
    spread = jnp.broadcast_to(gain_mine[None], (groups,) + gain_mine.shape)
    gain_gradient = jnp.sum(lax.all_to_all(spread, "dp", 0, 0, tiled=True), axis=0).reshape(width)
    return (mixed, grad_frames, grad_w_in[None], grad_w_out[None], grad_router, gain_gradient)


def solution(mesh):
    return jax.shard_map(
        functools.partial(on_device, mesh.shape["dp"]),
        mesh=mesh,
        in_specs=(
            P(("dp", "expert"), None),
            P(),
            P(),
            P("expert", "dp", None),
            P("expert", "dp", None),
            P(("dp", "expert"), None),
            P(("dp", "expert")),
            P(("dp", "expert"), None),
        ),
        out_specs=(
            P(("dp", "expert"), None),
            P(("dp", "expert"), None),
            P("expert", "dp", None),
            P("expert", "dp", None),
            P(),
            P(),
        ),
        check_vma=False,
    )
```

```python
import functools

import jax
import jax.numpy as jnp
from jax import lax
from jax.experimental import pallas as pl
from jax.experimental.pallas import tpu as pltpu
from jax.sharding import PartitionSpec as P

CAP = 18
MAIN = 16
EPS = 1e-05
LONG = 10**11
LANES = 128
NC = 2

f32 = jnp.float32
bf16 = jnp.bfloat16


def iota(shape, dim):
    return lax.broadcasted_iota(jnp.int32, shape, dim)


def indicator(condition):
    return jnp.where(condition, 1.0, 0.0).astype(bf16)


def matmul(a, b, **kw):
    return jnp.dot(a, b, preferred_element_type=f32, **kw)


def matmul_nt(a, b, **kw):
    return lax.dot_general(a, b, (((1,), (1,)), ((), ())), preferred_element_type=f32, **kw)


def extra_order(peers, pieces):
    rows = peers * MAIN
    i = iota((rows, rows), 0)
    j = iota((rows, rows), 1)
    return i, j, rows


def pack(rows, out_ref, peers):
    width = rows.shape[1]
    main = peers * MAIN
    out_ref[:, :width] = rows[:main]
    out_ref[:, width : width + LANES] = spread_pieces(rows[main:], peers)


def spread_pieces(extra, peers):
    pieces = extra.shape[1] // LANES
    stacked = jnp.concatenate([extra[:, p * LANES : (p + 1) * LANES] for p in range(pieces)], axis=0)
    i, j, _ = extra_order(peers, pieces)
    source = (i % pieces) * (2 * peers) + ((i // pieces) % 2) * peers + i // MAIN
    return matmul(indicator(j == source), stacked).astype(bf16)


def join_pieces(spread, peers):
    pieces = MAIN // 2
    i, j, _ = extra_order(peers, pieces)
    target = (i % peers) * MAIN + ((i // peers) % 2) * pieces + i // (2 * peers)
    stacked = matmul(indicator(j == target), spread).astype(bf16)
    return jnp.concatenate(
        [stacked[p * 2 * peers : (p + 1) * 2 * peers] for p in range(pieces)], axis=1
    )


def unpack(ref, peers):
    width = MAIN // 2 * LANES
    return ref[:, :width], join_pieces(ref[:, width : width + LANES], peers)


def unpack_into(packed_ref, rows_ref, peers):
    main, extra = unpack(packed_ref, peers)
    rows_ref[: peers * MAIN] = main
    rows_ref[peers * MAIN :] = extra


def layer_norm(frames_ref):
    floats = frames_ref[...].astype(f32)
    average = jnp.mean(floats, axis=1, keepdims=True)
    centered = floats - average
    inverse = lax.rsqrt(jnp.mean(centered * centered, axis=1, keepdims=True) + EPS)
    return floats, centered * inverse, inverse


def dispatch_kernel(peers, frames_ref, gain_ref, ids_ref, out_ref, normed_ref, place_ref):
    _, standardized, _ = layer_norm(frames_ref)
    normed = (standardized * gain_ref[...]).astype(bf16)
    normed_ref[...] = normed
    count = normed.shape[0]
    ids = ids_ref[...]
    expert = iota((peers, count), 0)
    first, second = expert == ids[0:1], expert == ids[1:2]
    earlier = indicator(iota((count, count), 0) < iota((count, count), 1))
    before = matmul(indicator(first | second), earlier)
    places = []
    for k, chosen in enumerate((first, second)):
        slot = jnp.sum(jnp.where(chosen, before, 0.0), axis=0, keepdims=True).astype(jnp.int32)
        e = ids[k : k + 1]
        places.append(
            jnp.where(slot < MAIN, e * MAIN + slot, peers * MAIN + (slot - MAIN) * peers + e)
        )
    place = jnp.concatenate(places, axis=0)
    place_ref[...] = place
    row = iota((peers * CAP, count), 0)
    select = indicator((row == place[0:1]) | (row == place[1:2]))
    pack(matmul(select, normed).astype(bf16), out_ref, peers)


def grads_kernel(peers, normed_ref, router_ref, ids_ref, mask_ref, place_ref, grad_ref, out_ref, meta_ref):
    logits = matmul_nt(router_ref[...], normed_ref[...])
    count = logits.shape[1]
    ids = ids_ref[...]
    place = place_ref[...]
    expert = iota((peers, count), 0)
    scores = [
        jax.nn.sigmoid(
            jnp.sum(jnp.where(expert == ids[k : k + 1], logits, 0.0), axis=0, keepdims=True)
        )
        for k in range(2)
    ]
    total = scores[0] + scores[1]
    live = mask_ref[...].astype(f32)
    weights = [live * s / total for s in scores]
    row = iota((peers * CAP, count), 0)
    here = [row == place[k : k + 1] for k in range(2)]
    scale = jnp.sum(
        jnp.where(here[0], weights[0], 0.0) + jnp.where(here[1], weights[1], 0.0),
        axis=1,
        keepdims=True,
    )
    rows = matmul(indicator(here[0] | here[1]), grad_ref[...])
    pack((rows * scale).astype(bf16), out_ref, peers)
    facts = jnp.concatenate(
        [
            place.astype(f32),
            ids.astype(f32),
            weights[0],
            weights[1],
            scores[0],
            scores[1],
            live,
            jnp.zeros((7, count), f32),
        ],
        axis=0,
    )
    padded = jnp.concatenate([facts, jnp.zeros((16, 256 - count), f32)], axis=1)
    meta_ref[...] = padded.T[:count]


def assemble(order_ref, pieces, out_ref):
    depth = pieces[0].shape[0]
    for j, piece in enumerate(pieces):
        out_ref[pl.ds(pl.multiple_of(order_ref[j] * depth, depth), depth)] = piece[...]


def first_kernel(peers, order_ref, packed_ref, *refs):
    pieces, (rows_ref, hidden_ref, derivative_ref, turned_ref, weights_ref) = refs[:-5], refs[-5:]
    depth = pieces[0].shape[0]

    @pl.when(pl.program_id(0) == 0)
    def _():
        unpack_into(packed_ref, rows_ref, peers)

    @pl.when(pl.program_id(0) == pl.num_programs(0) - 1)
    def _():
        for j in range(len(pieces)):
            columns = pl.ds(pl.multiple_of(order_ref[j] * depth, depth), depth)
            turned_ref[j * depth : (j + 1) * depth] = rows_ref[:, columns].T

    assemble(order_ref, pieces, weights_ref)
    pre = matmul(rows_ref[...], weights_ref[...])
    logistic = jax.nn.sigmoid(pre)
    hidden_ref[...] = (pre * logistic).astype(bf16)
    derivative_ref[...] = logistic * (1.0 + pre * (1.0 - logistic))


def second_kernel(peers, order_ref, hidden_ref, *refs):
    pieces, (out_ref, weights_ref, rows_ref) = refs[:-3], refs[-3:]
    step = pl.program_id(0)
    block = weights_ref.shape[1]
    columns = pl.ds(pl.multiple_of(step * block, block), block)
    assemble(order_ref, pieces, weights_ref)
    rows_ref[:, columns] = matmul(hidden_ref[...], weights_ref[...]).astype(bf16)

    @pl.when(step == pl.num_programs(0) - 1)
    def _():
        pack(rows_ref[...], out_ref, peers)


def outer_kernel(peers, order_ref, core_ref, packed_ref, hidden_ref, grads_ref, out_theirs_ref, out_mine_ref):
    block = out_mine_ref.shape[1]

    @pl.when(pl.program_id(0) == 0)
    def _():
        unpack_into(packed_ref, grads_ref, peers)

    product = matmul(hidden_ref[...].T, grads_ref[...]).astype(bf16)

    @pl.when(core_ref[0] == 0)
    def _():
        out_mine_ref[0] = product[:block]
        out_theirs_ref[0] = product[block:]

    @pl.when(core_ref[0] == 1)
    def _():
        out_theirs_ref[0] = product[:block]
        out_mine_ref[0] = product[block:]


def backward_kernel(
    peers, order_ref, holders_ref, grads_ref, derivative_ref, out_weights_ref, turned_ref, incoming_ref, gain_ref, *refs
):
    pieces, (in_theirs_ref, in_mine_ref, back_ref, gain_part_ref, rows_ref, in_ref) = refs[:-6], refs[-6:]
    step = pl.program_id(0)
    half, depth = in_mine_ref.shape[0], in_mine_ref.shape[1]
    assemble(holders_ref, pieces, in_ref)
    grads = grads_ref[...]
    grad_pre = (matmul_nt(grads, out_weights_ref[...]) * derivative_ref[...]).astype(bf16)
    product = matmul(turned_ref[...], grad_pre).astype(bf16)
    for j in range(half):
        in_mine_ref[j] = product[j * depth : (j + 1) * depth]
        in_theirs_ref[j] = product[(half + j) * depth : (half + j + 1) * depth]
    rows = matmul_nt(grad_pre, in_ref[...])

    @pl.when(step == 0)
    def _():
        rows_ref[...] = rows

    @pl.when(step > 0)
    def _():
        rows_ref[...] += rows

    @pl.when(step == pl.num_programs(0) - 1)
    def _():
        done = rows_ref[...].astype(bf16)
        pack(done, back_ref, peers)
        total = jnp.sum(done.astype(f32) * incoming_ref[...].astype(f32), axis=0, keepdims=True)
        gain_part_ref[...] = total / gain_ref[...]


def tally_kernel(peers, packed_ref, out_ref):
    rows = join_pieces(packed_ref[...], peers).astype(f32)
    out_ref[0:1] = jnp.sum(rows[:peers], axis=0, keepdims=True)
    out_ref[1:2] = jnp.sum(rows[peers:], axis=0, keepdims=True)


def pair_kernel(mine_ref, theirs_ref, kept_ref, *out_refs):
    kept_ref[...] = mine_ref[0].astype(f32) + theirs_ref[0].astype(f32)
    for k, out_ref in enumerate(out_refs):
        out_ref[...] = (mine_ref[k + 1].astype(f32) + theirs_ref[k + 1].astype(f32)).astype(bf16)


def total_kernel(first_ref, second_ref, *refs):
    ins, outs = refs[:-2], refs[-2:]
    count = len(ins) // 2
    for kept_ref, parts, out_ref in ((first_ref, ins[:count], outs[0]), (second_ref, ins[count:], outs[1])):
        total = kept_ref[...]
        for ref in parts:
            total += ref[...].astype(f32)
        out_ref[...] = total


def mix_kernel(
    peers, packed_ref, frames_ref, normed_ref, grad_ref, meta_ref, router_ref,
    packed_grads_ref, gain_expert_ref, mixed_ref, base_ref, out_ref,
):
    main, extra = unpack(packed_ref, peers)
    meta = meta_ref[...]
    column = [meta[:, k : k + 1] for k in range(9)]
    count = meta.shape[0]
    places = [c.astype(jnp.int32) for c in column[0:2]]
    experts = [c.astype(jnp.int32) for c in column[2:4]]
    weights, scores = column[4:6], column[6:8]
    cut = peers * MAIN
    lane = iota((count, cut), 1)
    lane_extra = iota((count, 2 * peers), 1) + cut
    grad = grad_ref[...].astype(f32)
    picked = [
        matmul(indicator(lane == p), main) + matmul(indicator(lane_extra == p), extra)
        for p in places
    ]
    floats, standardized, _ = layer_norm(frames_ref)
    mixed = floats + (weights[0] * picked[0] + weights[1] * picked[1])
    mixed_ref[...] = mixed.astype(bf16)
    grad_weight = [jnp.sum(grad * p, axis=1, keepdims=True) for p in picked]
    total = scores[0] + scores[1]
    gap = column[8] * (grad_weight[0] - grad_weight[1]) / (total * total)
    first = gap * scores[1] * scores[0] * (1.0 - scores[0])
    second = -gap * scores[0] * scores[1] * (1.0 - scores[1])
    which = iota((count, peers), 1)
    grad_logits = jnp.where(which == experts[0], first, 0.0) + jnp.where(
        which == experts[1], second, 0.0
    )
    base = matmul(grad_logits, router_ref[...].astype(f32), precision=lax.Precision.HIGHEST)
    base_ref[...] = base
    gain_part = gain_expert_ref[...] + jnp.sum(base * standardized, axis=0, keepdims=True)
    router_part = lax.dot_general(
        grad_logits,
        normed_ref[...].astype(f32),
        (((0,), (0,)), ((), ())),
        precision=lax.Precision.HIGHEST,
        preferred_element_type=f32,
    )
    sums = jnp.concatenate([router_part, jnp.broadcast_to(gain_part, router_part.shape)], axis=0)
    start = packed_grads_ref.shape[1]
    out_ref[:, :start] = packed_grads_ref[...]
    out_ref[:, start:] = spread_pieces(sums.astype(bf16), peers)


def finish_kernel(
    peers, packed_ref, frames_ref, gain_ref, grad_ref, meta_ref, base_ref, out_ref
):
    main, extra = unpack(packed_ref, peers)
    meta = meta_ref[...]
    count = meta.shape[0]
    places = [meta[:, k : k + 1].astype(jnp.int32) for k in range(2)]
    cut = peers * MAIN
    lane = iota((count, cut), 1)
    lane_extra = iota((count, 2 * peers), 1) + cut
    grad_moe = matmul(indicator((lane == places[0]) | (lane == places[1])), main) + matmul(
        indicator((lane_extra == places[0]) | (lane_extra == places[1])), extra
    )
    _, standardized, inverse = layer_norm(frames_ref)
    grad_normed = grad_moe + base_ref[...]
    g = grad_normed * gain_ref[...]
    statistic = inverse * (
        g
        - jnp.mean(g, axis=1, keepdims=True)
        - standardized * jnp.mean(g * standardized, axis=1, keepdims=True)
    )
    out_ref[...] = (grad_ref[...].astype(f32) + statistic).astype(bf16)


def call(kernel, name, *outs, grid=None, in_blocks=None, out_blocks=None, scratch=(), mib=58, order=(), cost=1):
    def spec(block, array):
        if block is None:
            dims = array.shape
            return pl.BlockSpec(dims, lambda i, *_: (0,) * len(dims))
        if block == "any":
            return pl.BlockSpec(memory_space=pl.ANY)
        return pl.BlockSpec(*block)

    def run(*args):
        ins = in_blocks if in_blocks is not None else [None] * len(args)
        ends = out_blocks if out_blocks is not None else [None] * len(outs)
        out_specs = [spec(b, o) for b, o in zip(ends, outs)]
        return pl.pallas_call(
            kernel,
            out_shape=outs if len(outs) > 1 else outs[0],
            grid_spec=pltpu.PrefetchScalarGridSpec(
                num_scalar_prefetch=len(order),
                grid=(grid or 1,),
                in_specs=[spec(b, a) for b, a in zip(ins, args)],
                out_specs=out_specs if len(outs) > 1 else out_specs[0],
                scratch_shapes=scratch,
            ),
            compiler_params=pltpu.CompilerParams(vmem_limit_bytes=mib * 1024 * 1024),
            cost_estimate=pl.CostEstimate(flops=cost, bytes_accessed=1, transcendentals=0),
            name=name,
        )(*order, *args)

    return run


def shape(*dims, dtype=bf16):
    return jax.ShapeDtypeStruct(dims, dtype)


def exchange(packed, peers):
    out = lax.all_to_all(
        packed.reshape(peers, MAIN, packed.shape[1]), "expert", split_axis=0, concat_axis=0, tiled=True
    )
    return out.reshape(packed.shape)


class Ring:
    def __init__(self, name, size, inner, fast):
        self.name, self.size, self.inner, self.fast = name, size, inner, fast
        self.length = inner if fast else size // inner
        place = lax.axis_index(name)
        self.place = place % inner if fast else place // inner

    def step(self, i, k):
        outer, within = i // self.inner, i % self.inner
        if self.fast:
            return outer * self.inner + (within + k) % self.inner
        return (outer + k) % self.length * self.inner + within

    def send(self, array, k):
        if k % self.length == 0:
            return array
        return lax.ppermute(array, self.name, [(i, self.step(i, k)) for i in range(self.size)])

    def behind(self):
        steps = jnp.arange(self.length, dtype=jnp.int32)
        return ((self.place - steps) % self.length).astype(jnp.int32)

    def ahead(self):
        steps = jnp.arange(self.length, dtype=jnp.int32)
        return ((self.place + steps) % self.length).astype(jnp.int32)


def pair_sums(mine, theirs, y, name, cost=1):
    count, depth, width = mine.shape
    steps = 2
    block = ((count, depth // steps, width), lambda i: (0, i, 0))
    flat = ((depth // steps, width), lambda i: (i, 0))
    kept, *sums = call(
        pair_kernel,
        name,
        shape(depth, width, dtype=f32),
        *[shape(depth, width)] * (count - 1),
        grid=steps,
        in_blocks=(block, block),
        out_blocks=(flat,) * count,
        cost=cost,
    )(mine, theirs)
    return kept, [y.send(part, -k - 1) for k, part in enumerate(sums)]


def total_sums(kept, parts):
    steps = 4
    flat = [((k.shape[0] // steps, k.shape[1]), lambda i: (i, 0)) for k in kept]
    count = len(parts[0])
    return call(
        total_kernel,
        "total",
        *[shape(*k.shape, dtype=f32) for k in kept],
        grid=steps,
        in_blocks=flat + [flat[0]] * count + [flat[1]] * count,
        out_blocks=flat,
    )(*kept, *parts[0], *parts[1])


def everyones(mine, axis, size):
    return lax.all_to_all(jnp.broadcast_to(mine[None], (size,) + mine.shape), axis, 0, 0, tiled=True)


def on_device(groups, frames, gain, router, w_in, w_out, expert_ids, frame_mask, out_grad):
    count, width = frames.shape
    peers = router.shape[1]
    rows = peers * CAP
    packed = shape(peers * MAIN, width + LANES)
    part = functools.partial
    gain = gain[None]
    router_rows = router.T
    ids = expert_ids.T
    core, y = Ring("dp", groups, NC, True), Ring("dp", groups, NC, False)
    behind = y.behind() * NC
    holders = jnp.concatenate([behind + core.place, behind + 1 - core.place])
    half = groups // 2

    sent, normed, place = call(
        part(dispatch_kernel, peers), "dispatch", packed, shape(count, width), shape(2, count, dtype=jnp.int32)
    )(frames, gain, ids)
    arrived = exchange(sent, peers)
    sent_grads, meta = call(
        part(grads_kernel, peers), "grads", packed, shape(count, 16, dtype=f32), cost=LONG
    )(normed, router_rows, ids, frame_mask[None], place, out_grad)
    pieces_in = [y.send(w_in[0], k) for k in range(half)]
    pieces_out = [y.send(w_out[0], k) if k != 2 else None for k in range(half)]
    later, _ = lax.optimization_barrier((w_out[0], pieces_in[2]))
    pieces_out[2] = y.send(later, 2)
    sent_grads, pieces_in, pieces_out[1], pieces_out[3] = lax.optimization_barrier(
        (sent_grads, pieces_in, pieces_out[1], pieces_out[3])
    )
    pieces_in += [core.send(piece, 1) for piece in pieces_in]
    arrived_grads = exchange(sent_grads, peers)

    inner = w_in.shape[2]
    block = 512
    column = ((rows, block), lambda i, order: (0, i))
    incoming, hidden, derivative, turned = call(
        part(first_kernel, peers),
        "first",
        shape(rows, width),
        shape(rows, inner),
        shape(rows, inner, dtype=f32),
        shape(width, rows),
        grid=inner // block,
        in_blocks=(None,) + (((width // groups, block), lambda i, order: (0, i)),) * groups,
        out_blocks=(None, column, column, None),
        scratch=[pltpu.VMEM((width, block), bf16)],
        order=(holders,),
    )(arrived, *pieces_in)
    hidden, pieces_out[2] = lax.optimization_barrier((hidden, pieces_out[2]))
    pieces_out += [core.send(piece, 1) for piece in pieces_out]
    block = 256
    expert_packed, weights_out = call(
        part(second_kernel, peers),
        "second",
        packed,
        shape(inner, width),
        grid=width // block,
        in_blocks=(None,) + (((inner // groups, block), lambda i, order: (0, i)),) * groups,
        out_blocks=(None, ((inner, block), lambda i, order: (0, i))),
        scratch=[pltpu.VMEM((rows, width), bf16)],
        order=(holders,),
    )(hidden, *pieces_out)
    expert_packed, arrived_grads = lax.optimization_barrier((expert_packed, arrived_grads))
    returned = exchange(expert_packed, peers)

    block = NC * inner // groups
    column = ((rows, block), lambda i, order, *_: (0, order[i]))
    split = ((half, width // groups, block), lambda i, order, *_: (0, 0, order[i]))
    whole = ((1, inner // groups, width), lambda i, *_: (i, 0, 0))
    grad_incoming, out_theirs, out_mine = call(
        part(outer_kernel, peers),
        "outer",
        shape(rows, width),
        *[shape(half, inner // groups, width)] * 2,
        grid=half,
        in_blocks=(None, column),
        out_blocks=(None, whole, whole),
        order=(y.behind(), core.place[None].astype(jnp.int32)),
    )(arrived_grads, hidden)
    in_theirs, in_mine, packed_grads, gain_expert = call(
        part(backward_kernel, peers),
        "backward",
        *[shape(half, width // groups, inner)] * 2,
        packed,
        shape(1, width, dtype=f32),
        grid=half,
        in_blocks=(
            None,
            column,
            ((block, width), lambda i, order, *_: (order[i], 0)),
            None,
            None,
            None,
        )
        + (((width // groups, block), lambda i, order, *_: (0, order[i])),) * groups,
        out_blocks=(split, split, None, None),
        scratch=[pltpu.VMEM((rows, width), f32), pltpu.VMEM((width, block), bf16)],
        order=(y.behind(), holders),
    )(grad_incoming, derivative, weights_out, turned, incoming, gain, *pieces_in)
    out_kept, out_parts = pair_sums(out_mine, core.send(out_theirs, 1), y, "out_pair")
    arrived_in, out_parts = lax.optimization_barrier((core.send(in_theirs, 1), out_parts))
    in_kept, in_parts = pair_sums(in_mine, arrived_in, y, "in_pair", cost=LONG)
    returned, packed_grads, out_kept = lax.optimization_barrier((returned, packed_grads, out_kept))

    mixed, base, sent_back = call(
        part(mix_kernel, peers),
        "mix",
        shape(count, width),
        shape(count, width, dtype=f32),
        shape(peers * MAIN, width + 2 * LANES),
        cost=LONG,
    )(returned, frames, normed, out_grad, meta, router_rows, packed_grads, gain_expert)
    back = exchange(sent_back, peers)
    back, out_parts, in_kept = lax.optimization_barrier((back, out_parts, in_kept))
    last = ((peers * MAIN, LANES), lambda i: (0, 1 + width // LANES))
    sums = call(part(tally_kernel, peers), "tally", shape(2, width, dtype=f32), in_blocks=(last,), mib=4)(back)
    sums = jnp.sum(everyones(sums.reshape(8, 2 * width // 8), "dp", groups), axis=0).reshape(2, width)
    grad_frames = call(part(finish_kernel, peers), "finish", shape(count, width))(
        back, frames, gain, out_grad, meta, base
    )
    sums, in_parts, grad_frames = lax.optimization_barrier((sums, in_parts, grad_frames))
    router_mine, gain_gradient = sums[0], sums[1]
    grad_router = everyones(router_mine.reshape(8, width // 8), "expert", peers).reshape(peers, width).T
    grad_w_out, grad_w_in = total_sums((out_kept, in_kept), (out_parts, in_parts))
    return (mixed, grad_frames, grad_w_in[None], grad_w_out[None], grad_router, gain_gradient)


def solution(mesh):
    return jax.shard_map(
        functools.partial(on_device, mesh.shape["dp"]),
        mesh=mesh,
        in_specs=(
            P(("dp", "expert"), None),
            P(),
            P(),
            P("expert", "dp", None),
            P("expert", "dp", None),
            P(("dp", "expert"), None),
            P(("dp", "expert")),
            P(("dp", "expert"), None),
        ),
        out_specs=(
            P(("dp", "expert"), None),
            P(("dp", "expert"), None),
            P("expert", "dp", None),
            P("expert", "dp", None),
            P(),
            P(),
        ),
        check_vma=False,
    )
```

```python
import functools

import jax
import jax.numpy as jnp
from jax import lax
from jax.experimental import pallas as pl
from jax.experimental.pallas import tpu as pltpu
from jax.sharding import PartitionSpec as P

CAP = 18
MAIN = 16
EPS = 1e-05
LONG = 10**11
LANES = 128
NC = 2

f32 = jnp.float32
bf16 = jnp.bfloat16


def iota(shape, dim):
    return lax.broadcasted_iota(jnp.int32, shape, dim)


def indicator(condition):
    return jnp.where(condition, 1.0, 0.0).astype(bf16)


def matmul(a, b, **kw):
    return jnp.dot(a, b, preferred_element_type=f32, **kw)


def matmul_nt(a, b, **kw):
    return lax.dot_general(a, b, (((1,), (1,)), ((), ())), preferred_element_type=f32, **kw)


def extra_order(peers, pieces):
    rows = peers * MAIN
    i = iota((rows, rows), 0)
    j = iota((rows, rows), 1)
    return i, j, rows


def pack(rows, out_ref, peers):
    width = rows.shape[1]
    main = peers * MAIN
    out_ref[:, :width] = rows[:main]
    out_ref[:, width : width + LANES] = spread_pieces(rows[main:], peers)


def pack_halves(rows, left_ref, right_ref, peers):
    main, cut = peers * MAIN, left_ref.shape[1]
    rest = rows.shape[1] - cut
    left_ref[...] = rows[:main, :cut]
    right_ref[:, :rest] = rows[:main, cut:]
    right_ref[:, rest : rest + LANES] = spread_pieces(rows[main:], peers)


def spread_pieces(extra, peers):
    pieces = extra.shape[1] // LANES
    stacked = jnp.concatenate([extra[:, p * LANES : (p + 1) * LANES] for p in range(pieces)], axis=0)
    i, j, _ = extra_order(peers, pieces)
    source = (i % pieces) * (2 * peers) + ((i // pieces) % 2) * peers + i // MAIN
    return matmul(indicator(j == source), stacked).astype(bf16)


def join_pieces(spread, peers):
    pieces = MAIN // 2
    i, j, _ = extra_order(peers, pieces)
    target = (i % peers) * MAIN + ((i // peers) % 2) * pieces + i // (2 * peers)
    stacked = matmul(indicator(j == target), spread).astype(bf16)
    return jnp.concatenate(
        [stacked[p * 2 * peers : (p + 1) * 2 * peers] for p in range(pieces)], axis=1
    )


def unpack(ref, peers):
    width = MAIN // 2 * LANES
    return ref[:, :width], join_pieces(ref[:, width : width + LANES], peers)


def unpack_into(packed_ref, rows_ref, peers):
    main, extra = unpack(packed_ref, peers)
    rows_ref[: peers * MAIN] = main
    rows_ref[peers * MAIN :] = extra


def layer_norm(frames_ref):
    floats = frames_ref[...].astype(f32)
    average = jnp.mean(floats, axis=1, keepdims=True)
    centered = floats - average
    inverse = lax.rsqrt(jnp.mean(centered * centered, axis=1, keepdims=True) + EPS)
    return floats, centered * inverse, inverse


def dispatch_kernel(peers, frames_ref, gain_ref, ids_ref, out_ref, normed_ref, place_ref):
    _, standardized, _ = layer_norm(frames_ref)
    normed = (standardized * gain_ref[...]).astype(bf16)
    normed_ref[...] = normed
    count = normed.shape[0]
    ids = ids_ref[...]
    expert = iota((peers, count), 0)
    first, second = expert == ids[0:1], expert == ids[1:2]
    earlier = indicator(iota((count, count), 0) < iota((count, count), 1))
    before = matmul(indicator(first | second), earlier)
    places = []
    for k, chosen in enumerate((first, second)):
        slot = jnp.sum(jnp.where(chosen, before, 0.0), axis=0, keepdims=True).astype(jnp.int32)
        e = ids[k : k + 1]
        places.append(
            jnp.where(slot < MAIN, e * MAIN + slot, peers * MAIN + (slot - MAIN) * peers + e)
        )
    place = jnp.concatenate(places, axis=0)
    place_ref[...] = place
    row = iota((peers * CAP, count), 0)
    select = indicator((row == place[0:1]) | (row == place[1:2]))
    pack(matmul(select, normed).astype(bf16), out_ref, peers)


def grads_kernel(peers, normed_ref, router_ref, ids_ref, mask_ref, place_ref, grad_ref, out_ref, meta_ref):
    logits = matmul_nt(router_ref[...], normed_ref[...])
    count = logits.shape[1]
    ids = ids_ref[...]
    place = place_ref[...]
    expert = iota((peers, count), 0)
    scores = [
        jax.nn.sigmoid(
            jnp.sum(jnp.where(expert == ids[k : k + 1], logits, 0.0), axis=0, keepdims=True)
        )
        for k in range(2)
    ]
    total = scores[0] + scores[1]
    live = mask_ref[...].astype(f32)
    weights = [live * s / total for s in scores]
    row = iota((peers * CAP, count), 0)
    here = [row == place[k : k + 1] for k in range(2)]
    scale = jnp.sum(
        jnp.where(here[0], weights[0], 0.0) + jnp.where(here[1], weights[1], 0.0),
        axis=1,
        keepdims=True,
    )
    rows = matmul(indicator(here[0] | here[1]), grad_ref[...])
    pack((rows * scale).astype(bf16), out_ref, peers)
    facts = jnp.concatenate(
        [
            place.astype(f32),
            ids.astype(f32),
            weights[0],
            weights[1],
            scores[0],
            scores[1],
            live,
            jnp.zeros((7, count), f32),
        ],
        axis=0,
    )
    padded = jnp.concatenate([facts, jnp.zeros((16, 256 - count), f32)], axis=1)
    meta_ref[...] = padded.T[:count]


def assemble(order_ref, pieces, out_ref):
    depth = pieces[0].shape[0]
    for j, piece in enumerate(pieces):
        out_ref[pl.ds(pl.multiple_of(order_ref[j] * depth, depth), depth)] = piece[...]


def first_kernel(peers, order_ref, packed_ref, *refs):
    pieces, (rows_ref, hidden_ref, derivative_ref, turned_ref, weights_ref) = refs[:-5], refs[-5:]
    depth = pieces[0].shape[0]

    @pl.when(pl.program_id(0) == 0)
    def _():
        unpack_into(packed_ref, rows_ref, peers)

    @pl.when(pl.program_id(0) == pl.num_programs(0) - 1)
    def _():
        for j in range(len(pieces)):
            columns = pl.ds(pl.multiple_of(order_ref[j] * depth, depth), depth)
            turned_ref[j * depth : (j + 1) * depth] = rows_ref[:, columns].T

    assemble(order_ref, pieces, weights_ref)
    pre = matmul(rows_ref[...], weights_ref[...])
    logistic = jax.nn.sigmoid(pre)
    hidden_ref[...] = (pre * logistic).astype(bf16)
    derivative_ref[...] = logistic * (1.0 + pre * (1.0 - logistic))


def second_kernel(peers, order_ref, hidden_ref, *refs):
    pieces, (out_ref, weights_ref, rows_ref) = refs[:-3], refs[-3:]
    step = pl.program_id(0)
    block = weights_ref.shape[1]
    columns = pl.ds(pl.multiple_of(step * block, block), block)
    assemble(order_ref, pieces, weights_ref)
    rows_ref[:, columns] = matmul(hidden_ref[...], weights_ref[...]).astype(bf16)

    @pl.when(step == pl.num_programs(0) - 1)
    def _():
        pack(rows_ref[...], out_ref, peers)


def outer_kernel(peers, order_ref, core_ref, packed_ref, hidden_ref, grads_ref, out_theirs_ref, out_mine_ref):
    block = out_mine_ref.shape[1]

    @pl.when(pl.program_id(0) == 0)
    def _():
        unpack_into(packed_ref, grads_ref, peers)

    product = matmul(hidden_ref[...].T, grads_ref[...]).astype(bf16)

    @pl.when(core_ref[0] == 0)
    def _():
        out_mine_ref[0] = product[:block]
        out_theirs_ref[0] = product[block:]

    @pl.when(core_ref[0] == 1)
    def _():
        out_theirs_ref[0] = product[:block]
        out_mine_ref[0] = product[block:]


def backward_kernel(
    peers, order_ref, holders_ref, grads_ref, derivative_ref, out_weights_ref, turned_ref, incoming_ref, gain_ref, *refs
):
    pieces, (in_theirs_ref, in_mine_ref, left_ref, right_ref, gain_part_ref, rows_ref, in_ref) = refs[:-7], refs[-7:]
    step = pl.program_id(0)
    half, depth = in_mine_ref.shape[0], in_mine_ref.shape[1]
    assemble(holders_ref, pieces, in_ref)
    grads = grads_ref[...]
    grad_pre = (matmul_nt(grads, out_weights_ref[...]) * derivative_ref[...]).astype(bf16)
    product = matmul(turned_ref[...], grad_pre).astype(bf16)
    for j in range(half):
        in_mine_ref[j] = product[j * depth : (j + 1) * depth]
        in_theirs_ref[j] = product[(half + j) * depth : (half + j + 1) * depth]
    rows = matmul_nt(grad_pre, in_ref[...])

    @pl.when(step == 0)
    def _():
        rows_ref[...] = rows

    @pl.when(step > 0)
    def _():
        rows_ref[...] += rows

    @pl.when(step == pl.num_programs(0) - 1)
    def _():
        done = rows_ref[...].astype(bf16)
        pack_halves(done, left_ref, right_ref, peers)
        total = jnp.sum(done.astype(f32) * incoming_ref[...].astype(f32), axis=0, keepdims=True)
        gain_part_ref[...] = total / gain_ref[...]


def tally_kernel(peers, packed_ref, out_ref):
    rows = join_pieces(packed_ref[...], peers).astype(f32)
    width = out_ref.shape[2]
    for k in range(2):
        total = jnp.sum(rows[k * peers : (k + 1) * peers], axis=0, keepdims=True)
        for j in range(4):
            out_ref[:, 4 * k + j] = jnp.broadcast_to(
                total[:, j * width : (j + 1) * width], (out_ref.shape[0], width)
            )


def sum_kernel(sums_ref, router_ref, gain_ref):
    total = jnp.sum(sums_ref[...], axis=0)
    width = total.shape[1]
    for j in range(4):
        gain_ref[:, j * width : (j + 1) * width] = total[4 + j : 5 + j]
    for j in range(8):
        row = total[j // 2 : j // 2 + 1, (j % 2) * LANES : (j % 2 + 1) * LANES]
        router_ref[:, j] = jnp.broadcast_to(row, (router_ref.shape[0], LANES))


def pair_kernel(mine_ref, theirs_ref, kept_ref, *out_refs):
    kept_ref[...] = mine_ref[0].astype(f32) + theirs_ref[0].astype(f32)
    for k, out_ref in enumerate(out_refs):
        out_ref[...] = (mine_ref[k + 1].astype(f32) + theirs_ref[k + 1].astype(f32)).astype(bf16)


def total_kernel(first_ref, second_ref, *refs):
    ins, outs = refs[:-2], refs[-2:]
    count = len(ins) // 2
    for kept_ref, parts, out_ref in ((first_ref, ins[:count], outs[0]), (second_ref, ins[count:], outs[1])):
        total = kept_ref[...]
        for ref in parts:
            total += ref[...].astype(f32)
        out_ref[...] = total


def picks(packed_ref, meta, peers):
    main, extra = unpack(packed_ref, peers)
    cut = peers * MAIN
    lane = iota((meta.shape[0], cut), 1)
    lane_extra = iota((meta.shape[0], 2 * peers), 1) + cut
    return [
        matmul(indicator(lane == place), main) + matmul(indicator(lane_extra == place), extra)
        for place in (meta[:, k : k + 1].astype(jnp.int32) for k in range(2))
    ]


def route_kernel(
    peers, packed_ref, normed_ref, grad_ref, meta_ref, router_ref, gain_ref, gain_expert_ref, _, out_ref, logits_ref
):
    meta = meta_ref[...]
    experts = [meta[:, k : k + 1].astype(jnp.int32) for k in (2, 3)]
    scores, live = [meta[:, k : k + 1] for k in (6, 7)], meta[:, 8:9]
    grad = grad_ref[...].astype(f32)
    grad_weight = [jnp.sum(grad * p, axis=1, keepdims=True) for p in picks(packed_ref, meta, peers)]
    total = scores[0] + scores[1]
    gap = live * (grad_weight[0] - grad_weight[1]) / (total * total)
    first = gap * scores[1] * scores[0] * (1.0 - scores[0])
    second = -gap * scores[0] * scores[1] * (1.0 - scores[1])
    which = iota((meta.shape[0], peers), 1)
    grad_logits = jnp.where(which == experts[0], first, 0.0) + jnp.where(
        which == experts[1], second, 0.0
    )
    logits_ref[...] = grad_logits
    router_part = lax.dot_general(
        grad_logits,
        normed_ref[...].astype(f32),
        (((0,), (0,)), ((), ())),
        precision=lax.Precision.HIGHEST,
        preferred_element_type=f32,
    )
    gain_part = jnp.sum(router_part * router_ref[...].astype(f32), axis=0, keepdims=True) / gain_ref[...]
    gain_part += gain_expert_ref[...]
    sums = jnp.concatenate([router_part, jnp.broadcast_to(gain_part, router_part.shape)], axis=0)
    out_ref[...] = spread_pieces(sums.astype(bf16), peers)


def mixed_kernel(peers, packed_ref, frames_ref, meta_ref, mixed_ref):
    meta = meta_ref[...]
    picked = picks(packed_ref, meta, peers)
    mixed_ref[...] = (
        frames_ref[...].astype(f32) + (meta[:, 4:5] * picked[0] + meta[:, 5:6] * picked[1])
    ).astype(bf16)


def finish_kernel(
    peers, left_ref, right_ref, frames_ref, gain_ref, grad_ref, meta_ref, logits_ref, router_ref, out_ref
):
    rest = frames_ref.shape[1] - left_ref.shape[1]
    main = jnp.concatenate([left_ref[...], right_ref[:, :rest]], axis=1)
    extra = join_pieces(right_ref[:, rest : rest + LANES], peers)
    meta = meta_ref[...]
    count = meta.shape[0]
    places = [meta[:, k : k + 1].astype(jnp.int32) for k in range(2)]
    cut = peers * MAIN
    lane = iota((count, cut), 1)
    lane_extra = iota((count, 2 * peers), 1) + cut
    grad_moe = matmul(indicator((lane == places[0]) | (lane == places[1])), main) + matmul(
        indicator((lane_extra == places[0]) | (lane_extra == places[1])), extra
    )
    _, standardized, inverse = layer_norm(frames_ref)
    grad_normed = grad_moe + matmul(
        logits_ref[...], router_ref[...].astype(f32), precision=lax.Precision.HIGHEST
    )
    g = grad_normed * gain_ref[...]
    statistic = inverse * (
        g
        - jnp.mean(g, axis=1, keepdims=True)
        - standardized * jnp.mean(g * standardized, axis=1, keepdims=True)
    )
    out_ref[...] = (grad_ref[...].astype(f32) + statistic).astype(bf16)


def call(kernel, name, *outs, grid=None, in_blocks=None, out_blocks=None, scratch=(), mib=58, order=(), cost=1, aliases=None):
    def spec(block, array):
        if block is None:
            dims = array.shape
            return pl.BlockSpec(dims, lambda i, *_: (0,) * len(dims))
        if block == "any":
            return pl.BlockSpec(memory_space=pl.ANY)
        return pl.BlockSpec(*block)

    def run(*args):
        ins = in_blocks if in_blocks is not None else [None] * len(args)
        ends = out_blocks if out_blocks is not None else [None] * len(outs)
        out_specs = [spec(b, o) for b, o in zip(ends, outs)]
        return pl.pallas_call(
            kernel,
            out_shape=outs if len(outs) > 1 else outs[0],
            grid_spec=pltpu.PrefetchScalarGridSpec(
                num_scalar_prefetch=len(order),
                grid=(grid or 1,),
                in_specs=[spec(b, a) for b, a in zip(ins, args)],
                out_specs=out_specs if len(outs) > 1 else out_specs[0],
                scratch_shapes=scratch,
            ),
            compiler_params=pltpu.CompilerParams(vmem_limit_bytes=mib * 1024 * 1024),
            cost_estimate=pl.CostEstimate(flops=cost, bytes_accessed=1, transcendentals=0),
            name=name,
            input_output_aliases=aliases or {},
        )(*order, *args)

    return run


def shape(*dims, dtype=bf16):
    return jax.ShapeDtypeStruct(dims, dtype)


def exchange(packed, peers):
    out = lax.all_to_all(
        packed.reshape(peers, MAIN, packed.shape[1]), "expert", split_axis=0, concat_axis=0, tiled=True
    )
    return out.reshape(packed.shape)


class Ring:
    def __init__(self, name, size, inner, fast):
        self.name, self.size, self.inner, self.fast = name, size, inner, fast
        self.length = inner if fast else size // inner
        place = lax.axis_index(name)
        self.place = place % inner if fast else place // inner

    def step(self, i, k):
        outer, within = i // self.inner, i % self.inner
        if self.fast:
            return outer * self.inner + (within + k) % self.inner
        return (outer + k) % self.length * self.inner + within

    def send(self, array, k):
        if k % self.length == 0:
            return array
        return lax.ppermute(array, self.name, [(i, self.step(i, k)) for i in range(self.size)])

    def behind(self):
        steps = jnp.arange(self.length, dtype=jnp.int32)
        return ((self.place - steps) % self.length).astype(jnp.int32)

    def ahead(self):
        steps = jnp.arange(self.length, dtype=jnp.int32)
        return ((self.place + steps) % self.length).astype(jnp.int32)


def pair_sums(mine, theirs, y, name, cost=1):
    count, depth, width = mine.shape
    steps = 2
    block = ((count, depth // steps, width), lambda i: (0, i, 0))
    flat = ((depth // steps, width), lambda i: (i, 0))
    kept, *sums = call(
        pair_kernel,
        name,
        shape(depth, width, dtype=f32),
        *[shape(depth, width)] * (count - 1),
        grid=steps,
        in_blocks=(block, block),
        out_blocks=(flat,) * count,
        cost=cost,
    )(mine, theirs)
    return kept, [y.send(part, -k - 1) for k, part in enumerate(sums)]


def total_sums(kept, parts):
    steps = 4
    flat = [((k.shape[0] // steps, k.shape[1]), lambda i: (i, 0)) for k in kept]
    count = len(parts[0])
    return call(
        total_kernel,
        "total",
        *[shape(*k.shape, dtype=f32) for k in kept],
        grid=steps,
        in_blocks=flat + [flat[0]] * count + [flat[1]] * count,
        out_blocks=flat,
    )(*kept, *parts[0], *parts[1])


def on_device(groups, frames, gain, router, w_in, w_out, expert_ids, frame_mask, out_grad):
    count, width = frames.shape
    peers = router.shape[1]
    rows = peers * CAP
    packed = shape(peers * MAIN, width + LANES)
    part = functools.partial
    gain = gain[None]
    router_rows = router.T
    ids = expert_ids.T
    core, y = Ring("dp", groups, NC, True), Ring("dp", groups, NC, False)
    behind = y.behind() * NC
    holders = jnp.concatenate([behind + core.place, behind + 1 - core.place])
    half = groups // 2

    sent, normed, place = call(
        part(dispatch_kernel, peers), "dispatch", packed, shape(count, width), shape(2, count, dtype=jnp.int32), cost=LONG
    )(frames, gain, ids)
    arrived = exchange(sent, peers)
    sent_grads, meta = call(
        part(grads_kernel, peers), "grads", packed, shape(count, 16, dtype=f32), cost=LONG
    )(normed, router_rows, ids, frame_mask[None], place, out_grad)
    pieces_in = [y.send(w_in[0], k) for k in range(half)]
    shard, _, pieces_in = lax.optimization_barrier((w_out[0], meta, pieces_in))
    pieces_in += [core.send(piece, 1) for piece in pieces_in]
    pieces_out = [y.send(shard, k) if k != 2 else None for k in range(half)]
    shard, _ = lax.optimization_barrier((shard, pieces_out[1]))
    pieces_out[2] = y.send(shard, 2)
    sent_grads, pieces_in, pieces_out[1], pieces_out[3] = lax.optimization_barrier(
        (sent_grads, pieces_in, pieces_out[1], pieces_out[3])
    )
    arrived_grads = exchange(sent_grads, peers)

    inner = w_in.shape[2]
    block = 512
    column = ((rows, block), lambda i, order: (0, i))
    incoming, hidden, derivative, turned = call(
        part(first_kernel, peers),
        "first",
        shape(rows, width),
        shape(rows, inner),
        shape(rows, inner, dtype=f32),
        shape(width, rows),
        grid=inner // block,
        in_blocks=(None,) + (((width // groups, block), lambda i, order: (0, i)),) * groups,
        out_blocks=(None, column, column, None),
        scratch=[pltpu.VMEM((width, block), bf16)],
        order=(holders,),
    )(arrived, *pieces_in)
    hidden, pieces_out[2] = lax.optimization_barrier((hidden, pieces_out[2]))
    pieces_out += [core.send(piece, 1) for piece in pieces_out]
    block = 256
    expert_packed, weights_out = call(
        part(second_kernel, peers),
        "second",
        packed,
        shape(inner, width),
        grid=width // block,
        in_blocks=(None,) + (((inner // groups, block), lambda i, order: (0, i)),) * groups,
        out_blocks=(None, ((inner, block), lambda i, order: (0, i))),
        scratch=[pltpu.VMEM((rows, width), bf16)],
        order=(holders,),
    )(hidden, *pieces_out)
    expert_packed, arrived_grads = lax.optimization_barrier((expert_packed, arrived_grads))
    returned = exchange(expert_packed, peers)

    block = NC * inner // groups
    column = ((rows, block), lambda i, order, *_: (0, order[i]))
    split = ((half, width // groups, block), lambda i, order, *_: (0, 0, order[i]))
    whole = ((1, inner // groups, width), lambda i, *_: (i, 0, 0))
    grad_incoming, out_theirs, out_mine = call(
        part(outer_kernel, peers),
        "outer",
        shape(rows, width),
        *[shape(half, inner // groups, width)] * 2,
        grid=half,
        in_blocks=(None, column),
        out_blocks=(None, whole, whole),
        order=(y.behind(), core.place[None].astype(jnp.int32)),
    )(arrived_grads, hidden)
    cut = width // 2 + LANES
    in_theirs, in_mine, left, right, gain_expert = call(
        part(backward_kernel, peers),
        "backward",
        *[shape(half, width // groups, inner)] * 2,
        *[shape(peers * MAIN, cut)] * 2,
        shape(1, width, dtype=f32),
        grid=half,
        in_blocks=(
            None,
            column,
            ((block, width), lambda i, order, *_: (order[i], 0)),
            None,
            None,
            None,
        )
        + (((width // groups, block), lambda i, order, *_: (0, order[i])),) * groups,
        out_blocks=(split, split, None, None, None),
        scratch=[pltpu.VMEM((rows, width), f32), pltpu.VMEM((width, block), bf16)],
        order=(y.behind(), holders),
    )(grad_incoming, derivative, weights_out, turned, incoming, gain, *pieces_in)
    arrived_out, _ = lax.optimization_barrier((core.send(out_theirs, 1), returned))
    out_kept, out_parts = pair_sums(out_mine, arrived_out, y, "out_pair")
    arrived_in, _ = lax.optimization_barrier((core.send(in_theirs, 1), out_kept))
    in_kept, in_parts = pair_sums(in_mine, arrived_in, y, "in_pair")
    back_left = exchange(left, peers)

    last = ((peers * MAIN, LANES), lambda i: (0, cut // LANES - 1))
    sent_back, grad_logits = call(
        part(route_kernel, peers),
        "route",
        shape(peers * MAIN, cut),
        shape(count, peers, dtype=f32),
        in_blocks=(None,) * 7 + ("any",),
        out_blocks=(last, None),
        cost=LONG,
        aliases={7: 0},
    )(returned, normed, out_grad, meta, router_rows, gain, gain_expert, right)
    sent_back, back_left, in_kept = lax.optimization_barrier((sent_back, back_left, in_kept))
    back = exchange(sent_back, peers)
    returned, out_parts = lax.optimization_barrier((returned, out_parts))
    mixed = call(part(mixed_kernel, peers), "mixed", shape(count, width), cost=LONG)(returned, frames, meta)
    back, out_parts, mixed = lax.optimization_barrier((back, out_parts, mixed))
    sums = call(
        part(tally_kernel, peers), "tally", shape(groups, 8, width // 4, dtype=f32), in_blocks=(last,), mib=4
    )(back)
    sums = lax.all_to_all(sums, "dp", 0, 0, tiled=True)
    grad_frames = call(part(finish_kernel, peers), "finish", shape(count, width))(
        back_left, back, frames, gain, out_grad, meta, grad_logits, router_rows
    )
    sums, in_parts, grad_frames = lax.optimization_barrier((sums, in_parts, grad_frames))
    router_mine, gain_gradient = call(
        sum_kernel, "sum", shape(peers, 8, width // 8, dtype=f32), shape(1, width, dtype=f32), mib=4
    )(sums)
    grad_router = lax.all_to_all(router_mine, "expert", 0, 0, tiled=True).reshape(peers, width).T
    grad_w_out, grad_w_in = total_sums((out_kept, in_kept), (out_parts, in_parts))
    return (mixed, grad_frames, grad_w_in[None], grad_w_out[None], grad_router, gain_gradient[0])


def solution(mesh):
    return jax.shard_map(
        functools.partial(on_device, mesh.shape["dp"]),
        mesh=mesh,
        in_specs=(
            P(("dp", "expert"), None),
            P(),
            P(),
            P("expert", "dp", None),
            P("expert", "dp", None),
            P(("dp", "expert"), None),
            P(("dp", "expert")),
            P(("dp", "expert"), None),
        ),
        out_specs=(
            P(("dp", "expert"), None),
            P(("dp", "expert"), None),
            P("expert", "dp", None),
            P("expert", "dp", None),
            P(),
            P(),
        ),
        check_vma=False,
    )
```

```python
import functools

import jax
import jax.numpy as jnp
from jax import lax
from jax.experimental import pallas as pl
from jax.experimental.pallas import tpu as pltpu
from jax.sharding import PartitionSpec as P

CAP = 18
MAIN = 16
EPS = 1e-05
LONG = 10**11
LANES = 128
NC = 2

f32 = jnp.float32
bf16 = jnp.bfloat16


def iota(shape, dim):
    return lax.broadcasted_iota(jnp.int32, shape, dim)


def indicator(condition):
    return jnp.where(condition, 1.0, 0.0).astype(bf16)


def matmul(a, b, **kw):
    return jnp.dot(a, b, preferred_element_type=f32, **kw)


def matmul_nt(a, b, **kw):
    return lax.dot_general(a, b, (((1,), (1,)), ((), ())), preferred_element_type=f32, **kw)


def extra_order(peers, pieces):
    rows = peers * MAIN
    i = iota((rows, rows), 0)
    j = iota((rows, rows), 1)
    return i, j, rows


def pack(rows, out_ref, peers):
    width = rows.shape[1]
    main = peers * MAIN
    out_ref[:, :width] = rows[:main]
    out_ref[:, width : width + LANES] = spread_pieces(rows[main:], peers)


def spread_pieces(extra, peers):
    pieces = extra.shape[1] // LANES
    stacked = jnp.concatenate([extra[:, p * LANES : (p + 1) * LANES] for p in range(pieces)], axis=0)
    i, j, _ = extra_order(peers, pieces)
    source = (i % pieces) * (2 * peers) + ((i // pieces) % 2) * peers + i // MAIN
    return matmul(indicator(j == source), stacked).astype(bf16)


def join_pieces(spread, peers):
    pieces = MAIN // 2
    i, j, _ = extra_order(peers, pieces)
    target = (i % peers) * MAIN + ((i // peers) % 2) * pieces + i // (2 * peers)
    stacked = matmul(indicator(j == target), spread).astype(bf16)
    return jnp.concatenate(
        [stacked[p * 2 * peers : (p + 1) * 2 * peers] for p in range(pieces)], axis=1
    )


def unpack(ref, peers):
    width = MAIN // 2 * LANES
    return ref[:, :width], join_pieces(ref[:, width : width + LANES], peers)


def unpack_into(packed_ref, rows_ref, peers):
    main, extra = unpack(packed_ref, peers)
    rows_ref[: peers * MAIN] = main
    rows_ref[peers * MAIN :] = extra


def layer_norm(frames_ref):
    floats = frames_ref[...].astype(f32)
    average = jnp.mean(floats, axis=1, keepdims=True)
    centered = floats - average
    inverse = lax.rsqrt(jnp.mean(centered * centered, axis=1, keepdims=True) + EPS)
    return floats, centered * inverse, inverse


def dispatch_kernel(peers, frames_ref, gain_ref, ids_ref, out_ref, normed_ref, place_ref):
    _, standardized, _ = layer_norm(frames_ref)
    normed = (standardized * gain_ref[...]).astype(bf16)
    normed_ref[...] = normed
    count = normed.shape[0]
    ids = ids_ref[...]
    expert = iota((peers, count), 0)
    first, second = expert == ids[0:1], expert == ids[1:2]
    earlier = indicator(iota((count, count), 0) < iota((count, count), 1))
    before = matmul(indicator(first | second), earlier)
    places = []
    for k, chosen in enumerate((first, second)):
        slot = jnp.sum(jnp.where(chosen, before, 0.0), axis=0, keepdims=True).astype(jnp.int32)
        e = ids[k : k + 1]
        places.append(
            jnp.where(slot < MAIN, e * MAIN + slot, peers * MAIN + (slot - MAIN) * peers + e)
        )
    place = jnp.concatenate(places, axis=0)
    place_ref[...] = place
    row = iota((peers * CAP, count), 0)
    select = indicator((row == place[0:1]) | (row == place[1:2]))
    pack(matmul(select, normed).astype(bf16), out_ref, peers)


def grads_kernel(peers, normed_ref, router_ref, ids_ref, mask_ref, place_ref, grad_ref, out_ref, meta_ref):
    logits = matmul_nt(router_ref[...], normed_ref[...])
    count = logits.shape[1]
    ids = ids_ref[...]
    place = place_ref[...]
    expert = iota((peers, count), 0)
    scores = [
        jax.nn.sigmoid(
            jnp.sum(jnp.where(expert == ids[k : k + 1], logits, 0.0), axis=0, keepdims=True)
        )
        for k in range(2)
    ]
    total = scores[0] + scores[1]
    live = mask_ref[...].astype(f32)
    weights = [live * s / total for s in scores]
    row = iota((peers * CAP, count), 0)
    here = [row == place[k : k + 1] for k in range(2)]
    scale = jnp.sum(
        jnp.where(here[0], weights[0], 0.0) + jnp.where(here[1], weights[1], 0.0),
        axis=1,
        keepdims=True,
    )
    rows = matmul(indicator(here[0] | here[1]), grad_ref[...])
    pack((rows * scale).astype(bf16), out_ref, peers)
    facts = jnp.concatenate(
        [
            place.astype(f32),
            ids.astype(f32),
            weights[0],
            weights[1],
            scores[0],
            scores[1],
            live,
            jnp.zeros((7, count), f32),
        ],
        axis=0,
    )
    padded = jnp.concatenate([facts, jnp.zeros((16, 256 - count), f32)], axis=1)
    meta_ref[...] = padded.T[:count]


def assemble(order_ref, pieces, out_ref):
    depth = pieces[0].shape[0]
    for j, piece in enumerate(pieces):
        out_ref[pl.ds(pl.multiple_of(order_ref[j] * depth, depth), depth)] = piece[...]


def first_kernel(peers, order_ref, packed_ref, *refs):
    pieces, (rows_ref, hidden_ref, derivative_ref, turned_ref, weights_ref) = refs[:-5], refs[-5:]
    depth = pieces[0].shape[0]

    @pl.when(pl.program_id(0) == 0)
    def _():
        unpack_into(packed_ref, rows_ref, peers)

    @pl.when(pl.program_id(0) == pl.num_programs(0) - 1)
    def _():
        for j in range(len(pieces)):
            columns = pl.ds(pl.multiple_of(order_ref[j] * depth, depth), depth)
            turned_ref[j * depth : (j + 1) * depth] = rows_ref[:, columns].T

    assemble(order_ref, pieces, weights_ref)
    pre = matmul(rows_ref[...], weights_ref[...])
    logistic = jax.nn.sigmoid(pre)
    hidden_ref[...] = (pre * logistic).astype(bf16)
    derivative_ref[...] = logistic * (1.0 + pre * (1.0 - logistic))


def second_kernel(peers, order_ref, hidden_ref, *refs):
    pieces, (out_ref, weights_ref, rows_ref) = refs[:-3], refs[-3:]
    step = pl.program_id(0)
    block = weights_ref.shape[1]
    columns = pl.ds(pl.multiple_of(step * block, block), block)
    assemble(order_ref, pieces, weights_ref)
    rows_ref[:, columns] = matmul(hidden_ref[...], weights_ref[...]).astype(bf16)

    @pl.when(step == pl.num_programs(0) - 1)
    def _():
        pack(rows_ref[...], out_ref, peers)


def outer_kernel(order_ref, core_ref, grads_ref, hidden_ref, *refs):
    theirs, mine_ref = refs[:-1], refs[-1]
    block = mine_ref.shape[1]
    step = pl.program_id(0)
    product = matmul(hidden_ref[...].T, grads_ref[...]).astype(bf16)
    first, second = product[:block], product[block:]
    mine_ref[0] = jnp.where(core_ref[0] == 0, first, second)
    other = jnp.where(core_ref[0] == 0, second, first)
    for k, ref in enumerate(theirs):

        @pl.when(step == k)
        def _(ref=ref):
            ref[...] = other


def backward_kernel(
    peers, order_ref, holders_ref, packed_ref, derivative_ref, out_weights_ref, turned_ref, incoming_ref, gain_ref, *refs
):
    pieces, (grads_ref, *in_theirs, in_mine_ref, back_ref, gain_part_ref, rows_ref, in_ref) = refs[:-10], refs[-10:]
    step = pl.program_id(0)
    half, depth = in_mine_ref.shape[0], in_mine_ref.shape[1]

    @pl.when(step == 0)
    def _():
        unpack_into(packed_ref, grads_ref, peers)

    assemble(holders_ref, pieces, in_ref)
    grads = grads_ref[...]
    grad_pre = (matmul_nt(grads, out_weights_ref[...]) * derivative_ref[...]).astype(bf16)
    product = matmul(turned_ref[...], grad_pre).astype(bf16)
    for j in range(half):
        in_mine_ref[j] = product[j * depth : (j + 1) * depth]
        in_theirs[j][...] = product[(half + j) * depth : (half + j + 1) * depth]
    rows = matmul_nt(grad_pre, in_ref[...])

    @pl.when(step == 0)
    def _():
        rows_ref[...] = rows

    @pl.when(step > 0)
    def _():
        rows_ref[...] += rows

    @pl.when(step == pl.num_programs(0) - 1)
    def _():
        done = rows_ref[...].astype(bf16)
        pack(done, back_ref, peers)
        total = jnp.sum(done.astype(f32) * incoming_ref[...].astype(f32), axis=0, keepdims=True)
        gain_part_ref[...] = total / gain_ref[...]


def tally_kernel(peers, packed_ref, out_ref):
    rows = join_pieces(packed_ref[...], peers).astype(f32)
    width = out_ref.shape[2]
    for k in range(2):
        total = jnp.sum(rows[k * peers : (k + 1) * peers], axis=0, keepdims=True)
        for j in range(4):
            out_ref[:, 4 * k + j] = jnp.broadcast_to(
                total[:, j * width : (j + 1) * width], (out_ref.shape[0], width)
            )


def sum_kernel(sums_ref, router_ref, gain_ref):
    total = jnp.sum(sums_ref[...], axis=0)
    width = total.shape[1]
    for j in range(4):
        gain_ref[:, j * width : (j + 1) * width] = total[4 + j : 5 + j]
    for j in range(8):
        row = total[j // 2 : j // 2 + 1, (j % 2) * LANES : (j % 2 + 1) * LANES]
        router_ref[:, j] = jnp.broadcast_to(row, (router_ref.shape[0], LANES))


def pair_kernel(count, mine_ref, *refs):
    theirs, kept_ref, outs = refs[:count], refs[count], refs[count + 1 :]
    kept_ref[...] = mine_ref[0].astype(f32) + theirs[0][...].astype(f32)
    for k, out_ref in enumerate(outs):
        out_ref[...] = (mine_ref[k + 1].astype(f32) + theirs[k + 1][...].astype(f32)).astype(bf16)


def total_kernel(first_ref, second_ref, *refs):
    ins, outs = refs[:-2], refs[-2:]
    count = len(ins) // 2
    for kept_ref, parts, out_ref in ((first_ref, ins[:count], outs[0]), (second_ref, ins[count:], outs[1])):
        total = kept_ref[...]
        for ref in parts:
            total += ref[...].astype(f32)
        out_ref[...] = total


def picks(packed_ref, meta, peers):
    main, extra = unpack(packed_ref, peers)
    cut = peers * MAIN
    lane = iota((meta.shape[0], cut), 1)
    lane_extra = iota((meta.shape[0], 2 * peers), 1) + cut
    return [
        matmul(indicator(lane == place), main) + matmul(indicator(lane_extra == place), extra)
        for place in (meta[:, k : k + 1].astype(jnp.int32) for k in range(2))
    ]


def route_kernel(
    peers, packed_ref, normed_ref, grad_ref, meta_ref, router_ref, gain_ref, gain_expert_ref, _, out_ref, logits_ref
):
    meta = meta_ref[...]
    experts = [meta[:, k : k + 1].astype(jnp.int32) for k in (2, 3)]
    scores, live = [meta[:, k : k + 1] for k in (6, 7)], meta[:, 8:9]
    grad = grad_ref[...].astype(f32)
    grad_weight = [jnp.sum(grad * p, axis=1, keepdims=True) for p in picks(packed_ref, meta, peers)]
    total = scores[0] + scores[1]
    gap = live * (grad_weight[0] - grad_weight[1]) / (total * total)
    first = gap * scores[1] * scores[0] * (1.0 - scores[0])
    second = -gap * scores[0] * scores[1] * (1.0 - scores[1])
    which = iota((meta.shape[0], peers), 1)
    grad_logits = jnp.where(which == experts[0], first, 0.0) + jnp.where(
        which == experts[1], second, 0.0
    )
    logits_ref[...] = grad_logits
    router_part = lax.dot_general(
        grad_logits,
        normed_ref[...].astype(f32),
        (((0,), (0,)), ((), ())),
        precision=lax.Precision.HIGHEST,
        preferred_element_type=f32,
    )
    gain_part = jnp.sum(router_part * router_ref[...].astype(f32), axis=0, keepdims=True) / gain_ref[...]
    gain_part += gain_expert_ref[...]
    sums = jnp.concatenate([router_part, jnp.broadcast_to(gain_part, router_part.shape)], axis=0)
    out_ref[...] = spread_pieces(sums.astype(bf16), peers)


def mixed_kernel(peers, packed_ref, frames_ref, meta_ref, mixed_ref):
    meta = meta_ref[...]
    picked = picks(packed_ref, meta, peers)
    mixed_ref[...] = (
        frames_ref[...].astype(f32) + (meta[:, 4:5] * picked[0] + meta[:, 5:6] * picked[1])
    ).astype(bf16)


def finish_kernel(
    peers, packed_ref, frames_ref, gain_ref, grad_ref, meta_ref, logits_ref, router_ref, out_ref
):
    main, extra = unpack(packed_ref, peers)
    meta = meta_ref[...]
    count = meta.shape[0]
    places = [meta[:, k : k + 1].astype(jnp.int32) for k in range(2)]
    cut = peers * MAIN
    lane = iota((count, cut), 1)
    lane_extra = iota((count, 2 * peers), 1) + cut
    grad_moe = matmul(indicator((lane == places[0]) | (lane == places[1])), main) + matmul(
        indicator((lane_extra == places[0]) | (lane_extra == places[1])), extra
    )
    _, standardized, inverse = layer_norm(frames_ref)
    grad_normed = grad_moe + matmul(
        logits_ref[...], router_ref[...].astype(f32), precision=lax.Precision.HIGHEST
    )
    g = grad_normed * gain_ref[...]
    statistic = inverse * (
        g
        - jnp.mean(g, axis=1, keepdims=True)
        - standardized * jnp.mean(g * standardized, axis=1, keepdims=True)
    )
    out_ref[...] = (grad_ref[...].astype(f32) + statistic).astype(bf16)


def call(kernel, name, *outs, grid=None, in_blocks=None, out_blocks=None, scratch=(), mib=58, order=(), cost=1, aliases=None):
    def spec(block, array):
        if block is None:
            dims = array.shape
            return pl.BlockSpec(dims, lambda i, *_: (0,) * len(dims))
        if block == "any":
            return pl.BlockSpec(memory_space=pl.ANY)
        return pl.BlockSpec(*block)

    def run(*args):
        ins = in_blocks if in_blocks is not None else [None] * len(args)
        ends = out_blocks if out_blocks is not None else [None] * len(outs)
        out_specs = [spec(b, o) for b, o in zip(ends, outs)]
        return pl.pallas_call(
            kernel,
            out_shape=outs if len(outs) > 1 else outs[0],
            grid_spec=pltpu.PrefetchScalarGridSpec(
                num_scalar_prefetch=len(order),
                grid=(grid or 1,),
                in_specs=[spec(b, a) for b, a in zip(ins, args)],
                out_specs=out_specs if len(outs) > 1 else out_specs[0],
                scratch_shapes=scratch,
            ),
            compiler_params=pltpu.CompilerParams(vmem_limit_bytes=mib * 1024 * 1024),
            cost_estimate=pl.CostEstimate(flops=cost, bytes_accessed=1, transcendentals=0),
            name=name,
            input_output_aliases=aliases or {},
        )(*order, *args)

    return run


def shape(*dims, dtype=bf16):
    return jax.ShapeDtypeStruct(dims, dtype)


def exchange(packed, peers):
    out = lax.all_to_all(
        packed.reshape(peers, MAIN, packed.shape[1]), "expert", split_axis=0, concat_axis=0, tiled=True
    )
    return out.reshape(packed.shape)


class Ring:
    def __init__(self, name, size, inner, fast):
        self.name, self.size, self.inner, self.fast = name, size, inner, fast
        self.length = inner if fast else size // inner
        place = lax.axis_index(name)
        self.place = place % inner if fast else place // inner

    def step(self, i, k):
        outer, within = i // self.inner, i % self.inner
        if self.fast:
            return outer * self.inner + (within + k) % self.inner
        return (outer + k) % self.length * self.inner + within

    def send(self, array, k):
        if k % self.length == 0:
            return array
        return lax.ppermute(array, self.name, [(i, self.step(i, k)) for i in range(self.size)])

    def behind(self):
        steps = jnp.arange(self.length, dtype=jnp.int32)
        return ((self.place - steps) % self.length).astype(jnp.int32)

    def ahead(self):
        steps = jnp.arange(self.length, dtype=jnp.int32)
        return ((self.place + steps) % self.length).astype(jnp.int32)


def pair_sums(mine, theirs, y, name, cost=1):
    count, depth, width = mine.shape
    steps = 2
    block = ((count, depth // steps, width), lambda i: (0, i, 0))
    flat = ((depth // steps, width), lambda i: (i, 0))
    kept, *sums = call(
        functools.partial(pair_kernel, count),
        name,
        shape(depth, width, dtype=f32),
        *[shape(depth, width)] * (count - 1),
        grid=steps,
        in_blocks=(block,) + (flat,) * count,
        out_blocks=(flat,) * count,
        cost=cost,
    )(mine, *theirs)
    return kept, [y.send(part, -k - 1) for k, part in enumerate(sums)]


def total_sums(kept, parts):
    steps = 4
    flat = [((k.shape[0] // steps, k.shape[1]), lambda i: (i, 0)) for k in kept]
    count = len(parts[0])
    return call(
        total_kernel,
        "total",
        *[shape(*k.shape, dtype=f32) for k in kept],
        grid=steps,
        in_blocks=flat + [flat[0]] * count + [flat[1]] * count,
        out_blocks=flat,
    )(*kept, *parts[0], *parts[1])


def on_device(groups, frames, gain, router, w_in, w_out, expert_ids, frame_mask, out_grad):
    count, width = frames.shape
    peers = router.shape[1]
    rows = peers * CAP
    packed = shape(peers * MAIN, width + LANES)
    part = functools.partial
    gain = gain[None]
    router_rows = router.T
    ids = expert_ids.T
    core, y = Ring("dp", groups, NC, True), Ring("dp", groups, NC, False)
    behind = y.behind() * NC
    holders = jnp.concatenate([behind + core.place, behind + 1 - core.place])
    half = groups // 2

    sent, normed, place = call(
        part(dispatch_kernel, peers), "dispatch", packed, shape(count, width), shape(2, count, dtype=jnp.int32), cost=LONG
    )(frames, gain, ids)
    arrived = exchange(sent, peers)
    sent_grads, meta = call(
        part(grads_kernel, peers), "grads", packed, shape(count, 16, dtype=f32), cost=LONG
    )(normed, router_rows, ids, frame_mask[None], place, out_grad)
    pieces_in = [y.send(w_in[0], k) for k in range(half)]
    shard, _, pieces_in = lax.optimization_barrier((w_out[0], meta, pieces_in))
    pieces_in += [core.send(piece, 1) for piece in pieces_in]
    pieces_out = [y.send(shard, k) if k != 2 else None for k in range(half)]
    shard, _ = lax.optimization_barrier((shard, pieces_out[1]))
    pieces_out[2] = y.send(shard, 2)
    sent_grads, pieces_in, pieces_out[1], pieces_out[3] = lax.optimization_barrier(
        (sent_grads, pieces_in, pieces_out[1], pieces_out[3])
    )
    arrived_grads = exchange(sent_grads, peers)

    inner = w_in.shape[2]
    block = 512
    column = ((rows, block), lambda i, order: (0, i))
    incoming, hidden, derivative, turned = call(
        part(first_kernel, peers),
        "first",
        shape(rows, width),
        shape(rows, inner),
        shape(rows, inner, dtype=f32),
        shape(width, rows),
        grid=inner // block,
        in_blocks=(None,) + (((width // groups, block), lambda i, order: (0, i)),) * groups,
        out_blocks=(None, column, column, None),
        scratch=[pltpu.VMEM((width, block), bf16)],
        order=(holders,),
    )(arrived, *pieces_in)
    hidden, pieces_out[2] = lax.optimization_barrier((hidden, pieces_out[2]))
    pieces_out += [core.send(piece, 1) for piece in pieces_out]
    block = 256
    expert_packed, weights_out = call(
        part(second_kernel, peers),
        "second",
        packed,
        shape(inner, width),
        grid=width // block,
        in_blocks=(None,) + (((inner // groups, block), lambda i, order: (0, i)),) * groups,
        out_blocks=(None, ((inner, block), lambda i, order: (0, i))),
        scratch=[pltpu.VMEM((rows, width), bf16)],
        order=(holders,),
    )(hidden, *pieces_out)
    expert_packed, arrived_grads = lax.optimization_barrier((expert_packed, arrived_grads))
    returned = exchange(expert_packed, peers)

    block = NC * inner // groups
    column = ((rows, block), lambda i, order, *_: (0, order[i]))
    split = ((half, width // groups, block), lambda i, order, *_: (0, 0, order[i]))
    whole = ((1, inner // groups, width), lambda i, *_: (i, 0, 0))
    grad_incoming, *in_theirs, in_mine, packed_grads, gain_expert = call(
        part(backward_kernel, peers),
        "backward",
        shape(rows, width),
        *[shape(width // groups, inner)] * half,
        shape(half, width // groups, inner),
        shape(peers * MAIN, width + 2 * LANES),
        shape(1, width, dtype=f32),
        grid=half,
        in_blocks=(
            None,
            column,
            ((block, width), lambda i, order, *_: (order[i], 0)),
            None,
            None,
            None,
        )
        + (((width // groups, block), lambda i, order, *_: (0, order[i])),) * groups,
        out_blocks=(None,) + (((width // groups, block), lambda i, order, *_: (0, order[i])),) * half + (split, (packed.shape, lambda i, *_: (0, 0)), None),
        scratch=[pltpu.VMEM((rows, width), f32), pltpu.VMEM((width, block), bf16)],
        order=(y.behind(), holders),
    )(arrived_grads, derivative, weights_out, turned, incoming, gain, *pieces_in)
    in_kept, in_parts = pair_sums(in_mine, [core.send(part, 1) for part in in_theirs], y, "in_pair")
    returned, packed_grads, in_kept = lax.optimization_barrier((returned, packed_grads, in_kept))

    last = ((peers * MAIN, LANES), lambda i: (0, 1 + width // LANES))
    sent_back, grad_logits = call(
        part(route_kernel, peers),
        "route",
        shape(peers * MAIN, width + 2 * LANES),
        shape(count, peers, dtype=f32),
        in_blocks=(None,) * 7 + ("any",),
        out_blocks=(last, None),
        aliases={7: 0},
    )(returned, normed, out_grad, meta, router_rows, gain, gain_expert, packed_grads)
    returned, sent_back = lax.optimization_barrier((returned, sent_back))
    back = exchange(sent_back, peers)
    grad_incoming, _ = lax.optimization_barrier((grad_incoming, grad_logits))
    *out_theirs, out_mine = call(
        outer_kernel,
        "outer",
        *[shape(inner // groups, width)] * half,
        shape(half, inner // groups, width),
        grid=half,
        in_blocks=(None, column),
        out_blocks=(None,) * half + (whole,),
        order=(y.behind(), core.place[None].astype(jnp.int32)),
        cost=LONG,
    )(grad_incoming, hidden)
    arrived_out, in_parts = lax.optimization_barrier(([core.send(part, 1) for part in out_theirs], in_parts))
    out_kept, out_parts = pair_sums(out_mine, arrived_out, y, "out_pair")
    mixed = call(part(mixed_kernel, peers), "mixed", shape(count, width))(returned, frames, meta)
    back, out_kept, mixed = lax.optimization_barrier((back, out_kept, mixed))
    sums = call(
        part(tally_kernel, peers), "tally", shape(groups, 8, width // 4, dtype=f32), in_blocks=(last,), mib=4
    )(back)
    sums = lax.all_to_all(sums, "dp", 0, 0, tiled=True)
    grad_frames = call(part(finish_kernel, peers), "finish", shape(count, width))(
        back, frames, gain, out_grad, meta, grad_logits, router_rows
    )
    sums, grad_frames = lax.optimization_barrier((sums, grad_frames))
    router_mine, gain_gradient = call(
        sum_kernel, "sum", shape(peers, 8, width // 8, dtype=f32), shape(1, width, dtype=f32), mib=4
    )(sums)
    grad_router = lax.all_to_all(router_mine, "expert", 0, 0, tiled=True).reshape(peers, width).T
    grad_w_out, grad_w_in = total_sums((out_kept, in_kept), (out_parts, in_parts))
    return (mixed, grad_frames, grad_w_in[None], grad_w_out[None], grad_router, gain_gradient[0])


def solution(mesh):
    return jax.shard_map(
        functools.partial(on_device, mesh.shape["dp"]),
        mesh=mesh,
        in_specs=(
            P(("dp", "expert"), None),
            P(),
            P(),
            P("expert", "dp", None),
            P("expert", "dp", None),
            P(("dp", "expert"), None),
            P(("dp", "expert")),
            P(("dp", "expert"), None),
        ),
        out_specs=(
            P(("dp", "expert"), None),
            P(("dp", "expert"), None),
            P("expert", "dp", None),
            P("expert", "dp", None),
            P(),
            P(),
        ),
        check_vma=False,
    )
```

```python
import functools

import jax
import jax.numpy as jnp
from jax import lax
from jax.experimental import pallas as pl
from jax.experimental.pallas import tpu as pltpu
from jax.sharding import PartitionSpec as P

CAP = 18
MAIN = 16
EPS = 1e-05
LONG = 10**11
LANES = 128
NC = 2

f32 = jnp.float32
bf16 = jnp.bfloat16


def iota(shape, dim):
    return lax.broadcasted_iota(jnp.int32, shape, dim)


def indicator(condition):
    return jnp.where(condition, 1.0, 0.0).astype(bf16)


def matmul(a, b, **kw):
    return jnp.dot(a, b, preferred_element_type=f32, **kw)


def matmul_nt(a, b, **kw):
    return lax.dot_general(a, b, (((1,), (1,)), ((), ())), preferred_element_type=f32, **kw)


def extra_order(peers, pieces):
    rows = peers * MAIN
    i = iota((rows, rows), 0)
    j = iota((rows, rows), 1)
    return i, j, rows


def pack(rows, out_ref, peers):
    width = rows.shape[1]
    main = peers * MAIN
    out_ref[:, :width] = rows[:main]
    out_ref[:, width : width + LANES] = spread_pieces(rows[main:], peers)


def spread_pieces(extra, peers):
    pieces = extra.shape[1] // LANES
    stacked = jnp.concatenate([extra[:, p * LANES : (p + 1) * LANES] for p in range(pieces)], axis=0)
    i, j, _ = extra_order(peers, pieces)
    source = (i % pieces) * (2 * peers) + ((i // pieces) % 2) * peers + i // MAIN
    return matmul(indicator(j == source), stacked).astype(bf16)


def join_pieces(spread, peers):
    pieces = MAIN // 2
    i, j, _ = extra_order(peers, pieces)
    target = (i % peers) * MAIN + ((i // peers) % 2) * pieces + i // (2 * peers)
    stacked = matmul(indicator(j == target), spread).astype(bf16)
    return jnp.concatenate(
        [stacked[p * 2 * peers : (p + 1) * 2 * peers] for p in range(pieces)], axis=1
    )


def unpack(ref, peers):
    width = MAIN // 2 * LANES
    return ref[:, :width], join_pieces(ref[:, width : width + LANES], peers)


def unpack_into(packed_ref, rows_ref, peers):
    main, extra = unpack(packed_ref, peers)
    rows_ref[: peers * MAIN] = main
    rows_ref[peers * MAIN :] = extra


def layer_norm(frames_ref):
    floats = frames_ref[...].astype(f32)
    average = jnp.mean(floats, axis=1, keepdims=True)
    centered = floats - average
    inverse = lax.rsqrt(jnp.mean(centered * centered, axis=1, keepdims=True) + EPS)
    return floats, centered * inverse, inverse


def dispatch_kernel(peers, frames_ref, gain_ref, ids_ref, out_ref, normed_ref, place_ref):
    _, standardized, _ = layer_norm(frames_ref)
    normed = (standardized * gain_ref[...]).astype(bf16)
    normed_ref[...] = normed
    count = normed.shape[0]
    ids = ids_ref[...]
    expert = iota((peers, count), 0)
    first, second = expert == ids[0:1], expert == ids[1:2]
    earlier = indicator(iota((count, count), 0) < iota((count, count), 1))
    before = matmul(indicator(first | second), earlier)
    places = []
    for k, chosen in enumerate((first, second)):
        slot = jnp.sum(jnp.where(chosen, before, 0.0), axis=0, keepdims=True).astype(jnp.int32)
        e = ids[k : k + 1]
        places.append(
            jnp.where(slot < MAIN, e * MAIN + slot, peers * MAIN + (slot - MAIN) * peers + e)
        )
    place = jnp.concatenate(places, axis=0)
    place_ref[...] = place
    row = iota((peers * CAP, count), 0)
    select = indicator((row == place[0:1]) | (row == place[1:2]))
    pack(matmul(select, normed).astype(bf16), out_ref, peers)


def grads_kernel(peers, normed_ref, router_ref, ids_ref, mask_ref, place_ref, grad_ref, out_ref, meta_ref):
    logits = matmul_nt(router_ref[...], normed_ref[...])
    count = logits.shape[1]
    ids = ids_ref[...]
    place = place_ref[...]
    expert = iota((peers, count), 0)
    scores = [
        jax.nn.sigmoid(
            jnp.sum(jnp.where(expert == ids[k : k + 1], logits, 0.0), axis=0, keepdims=True)
        )
        for k in range(2)
    ]
    total = scores[0] + scores[1]
    live = mask_ref[...].astype(f32)
    weights = [live * s / total for s in scores]
    row = iota((peers * CAP, count), 0)
    here = [row == place[k : k + 1] for k in range(2)]
    scale = jnp.sum(
        jnp.where(here[0], weights[0], 0.0) + jnp.where(here[1], weights[1], 0.0),
        axis=1,
        keepdims=True,
    )
    rows = matmul(indicator(here[0] | here[1]), grad_ref[...])
    pack((rows * scale).astype(bf16), out_ref, peers)
    facts = jnp.concatenate(
        [
            place.astype(f32),
            ids.astype(f32),
            weights[0],
            weights[1],
            scores[0],
            scores[1],
            live,
            jnp.zeros((7, count), f32),
        ],
        axis=0,
    )
    padded = jnp.concatenate([facts, jnp.zeros((16, 256 - count), f32)], axis=1)
    meta_ref[...] = padded.T[:count]


def assemble(order_ref, pieces, out_ref):
    depth = pieces[0].shape[0]
    for j, piece in enumerate(pieces):
        out_ref[pl.ds(pl.multiple_of(order_ref[j] * depth, depth), depth)] = piece[...]


def first_kernel(peers, order_ref, packed_ref, *refs):
    pieces, (rows_ref, hidden_ref, derivative_ref, turned_ref, weights_ref) = refs[:-5], refs[-5:]
    depth = pieces[0].shape[0]

    @pl.when(pl.program_id(0) == 0)
    def _():
        unpack_into(packed_ref, rows_ref, peers)

    @pl.when(pl.program_id(0) == pl.num_programs(0) - 1)
    def _():
        for j in range(len(pieces)):
            columns = pl.ds(pl.multiple_of(order_ref[j] * depth, depth), depth)
            turned_ref[j * depth : (j + 1) * depth] = rows_ref[:, columns].T

    assemble(order_ref, pieces, weights_ref)
    pre = matmul(rows_ref[...], weights_ref[...])
    logistic = jax.nn.sigmoid(pre)
    hidden_ref[...] = (pre * logistic).astype(bf16)
    derivative_ref[...] = logistic * (1.0 + pre * (1.0 - logistic))


def second_kernel(peers, order_ref, hidden_ref, *refs):
    pieces, (out_ref, weights_ref, rows_ref) = refs[:-3], refs[-3:]
    step = pl.program_id(0)
    block = weights_ref.shape[1]
    columns = pl.ds(pl.multiple_of(step * block, block), block)
    assemble(order_ref, pieces, weights_ref)
    rows_ref[:, columns] = matmul(hidden_ref[...], weights_ref[...]).astype(bf16)

    @pl.when(step == pl.num_programs(0) - 1)
    def _():
        pack(rows_ref[...], out_ref, peers)


def outer_kernel(order_ref, core_ref, grads_ref, hidden_ref, *refs):
    theirs, mine_ref = refs[:-1], refs[-1]
    block = mine_ref.shape[1]
    step = pl.program_id(0)
    product = matmul(hidden_ref[...].T, grads_ref[...]).astype(bf16)
    first, second = product[:block], product[block:]
    mine_ref[0] = jnp.where(core_ref[0] == 0, first, second)
    other = jnp.where(core_ref[0] == 0, second, first)
    for k, ref in enumerate(theirs):

        @pl.when(step == k)
        def _(ref=ref):
            ref[...] = other


def backward_kernel(
    peers, order_ref, holders_ref, packed_ref, derivative_ref, out_weights_ref, turned_ref, incoming_ref, gain_ref, *refs
):
    pieces, (grads_ref, *in_theirs, in_mine_ref, back_ref, gain_part_ref, rows_ref, in_ref) = refs[:-10], refs[-10:]
    step = pl.program_id(0)
    half, depth = in_mine_ref.shape[0], in_mine_ref.shape[1]

    @pl.when(step == 0)
    def _():
        unpack_into(packed_ref, grads_ref, peers)

    assemble(holders_ref, pieces, in_ref)
    grads = grads_ref[...]
    grad_pre = (matmul_nt(grads, out_weights_ref[...]) * derivative_ref[...]).astype(bf16)
    product = matmul(turned_ref[...], grad_pre).astype(bf16)
    for j in range(half):
        in_mine_ref[j] = product[j * depth : (j + 1) * depth]
        in_theirs[j][...] = product[(half + j) * depth : (half + j + 1) * depth]
    rows = matmul_nt(grad_pre, in_ref[...])

    @pl.when(step == 0)
    def _():
        rows_ref[...] = rows

    @pl.when(step > 0)
    def _():
        rows_ref[...] += rows

    @pl.when(step == pl.num_programs(0) - 1)
    def _():
        done = rows_ref[...].astype(bf16)
        pack(done, back_ref, peers)
        total = jnp.sum(done.astype(f32) * incoming_ref[...].astype(f32), axis=0, keepdims=True)
        gain_part_ref[...] = total / gain_ref[...]


def tally_kernel(peers, packed_ref, out_ref):
    rows = join_pieces(packed_ref[...], peers).astype(f32)
    width = out_ref.shape[2]
    for k in range(2):
        total = jnp.sum(rows[k * peers : (k + 1) * peers], axis=0, keepdims=True)
        for j in range(4):
            out_ref[:, 4 * k + j] = jnp.broadcast_to(
                total[:, j * width : (j + 1) * width], (out_ref.shape[0], width)
            )


def sum_kernel(sums_ref, router_ref, gain_ref):
    total = jnp.sum(sums_ref[...], axis=0)
    width = total.shape[1]
    for j in range(4):
        gain_ref[:, j * width : (j + 1) * width] = total[4 + j : 5 + j]
    for j in range(8):
        row = total[j // 2 : j // 2 + 1, (j % 2) * LANES : (j % 2 + 1) * LANES]
        router_ref[:, j] = jnp.broadcast_to(row, (router_ref.shape[0], LANES))


def pair_kernel(count, mine_ref, *refs):
    theirs, kept_ref, outs = refs[:count], refs[count], refs[count + 1 :]
    kept_ref[...] = mine_ref[0].astype(f32) + theirs[0][...].astype(f32)
    for k, out_ref in enumerate(outs):
        out_ref[...] = (mine_ref[k + 1].astype(f32) + theirs[k + 1][...].astype(f32)).astype(bf16)


def total_kernel(first_ref, second_ref, *refs):
    ins, outs = refs[:-2], refs[-2:]
    count = len(ins) // 2
    for kept_ref, parts, out_ref in ((first_ref, ins[:count], outs[0]), (second_ref, ins[count:], outs[1])):
        total = kept_ref[...]
        for ref in parts:
            total += ref[...].astype(f32)
        out_ref[...] = total


def picks(packed_ref, meta, peers):
    main, extra = unpack(packed_ref, peers)
    cut = peers * MAIN
    lane = iota((meta.shape[0], cut), 1)
    lane_extra = iota((meta.shape[0], 2 * peers), 1) + cut
    return [
        matmul(indicator(lane == place), main) + matmul(indicator(lane_extra == place), extra)
        for place in (meta[:, k : k + 1].astype(jnp.int32) for k in range(2))
    ]


def route_kernel(
    peers, packed_ref, normed_ref, grad_ref, meta_ref, router_ref, gain_ref, gain_expert_ref, _, out_ref, logits_ref
):
    meta = meta_ref[...]
    experts = [meta[:, k : k + 1].astype(jnp.int32) for k in (2, 3)]
    scores, live = [meta[:, k : k + 1] for k in (6, 7)], meta[:, 8:9]
    grad = grad_ref[...].astype(f32)
    grad_weight = [jnp.sum(grad * p, axis=1, keepdims=True) for p in picks(packed_ref, meta, peers)]
    total = scores[0] + scores[1]
    gap = live * (grad_weight[0] - grad_weight[1]) / (total * total)
    first = gap * scores[1] * scores[0] * (1.0 - scores[0])
    second = -gap * scores[0] * scores[1] * (1.0 - scores[1])
    which = iota((meta.shape[0], peers), 1)
    grad_logits = jnp.where(which == experts[0], first, 0.0) + jnp.where(
        which == experts[1], second, 0.0
    )
    logits_ref[...] = grad_logits
    router_part = lax.dot_general(
        grad_logits,
        normed_ref[...].astype(f32),
        (((0,), (0,)), ((), ())),
        precision=lax.Precision.HIGHEST,
        preferred_element_type=f32,
    )
    gain_part = jnp.sum(router_part * router_ref[...].astype(f32), axis=0, keepdims=True) / gain_ref[...]
    gain_part += gain_expert_ref[...]
    sums = jnp.concatenate([router_part, jnp.broadcast_to(gain_part, router_part.shape)], axis=0)
    out_ref[...] = spread_pieces(sums.astype(bf16), peers)


def mixed_kernel(peers, packed_ref, frames_ref, meta_ref, mixed_ref):
    meta = meta_ref[...]
    picked = picks(packed_ref, meta, peers)
    mixed_ref[...] = (
        frames_ref[...].astype(f32) + (meta[:, 4:5] * picked[0] + meta[:, 5:6] * picked[1])
    ).astype(bf16)


def finish_kernel(
    peers, packed_ref, frames_ref, gain_ref, grad_ref, meta_ref, logits_ref, router_ref, out_ref
):
    main, extra = unpack(packed_ref, peers)
    meta = meta_ref[...]
    count = meta.shape[0]
    places = [meta[:, k : k + 1].astype(jnp.int32) for k in range(2)]
    cut = peers * MAIN
    lane = iota((count, cut), 1)
    lane_extra = iota((count, 2 * peers), 1) + cut
    grad_moe = matmul(indicator((lane == places[0]) | (lane == places[1])), main) + matmul(
        indicator((lane_extra == places[0]) | (lane_extra == places[1])), extra
    )
    _, standardized, inverse = layer_norm(frames_ref)
    grad_normed = grad_moe + matmul(
        logits_ref[...], router_ref[...].astype(f32), precision=lax.Precision.HIGHEST
    )
    g = grad_normed * gain_ref[...]
    statistic = inverse * (
        g
        - jnp.mean(g, axis=1, keepdims=True)
        - standardized * jnp.mean(g * standardized, axis=1, keepdims=True)
    )
    out_ref[...] = (grad_ref[...].astype(f32) + statistic).astype(bf16)


def call(kernel, name, *outs, grid=None, in_blocks=None, out_blocks=None, scratch=(), mib=58, order=(), cost=1, aliases=None):
    def spec(block, array):
        if block is None:
            dims = array.shape
            return pl.BlockSpec(dims, lambda i, *_: (0,) * len(dims))
        if block == "any":
            return pl.BlockSpec(memory_space=pl.ANY)
        return pl.BlockSpec(*block)

    def run(*args):
        ins = in_blocks if in_blocks is not None else [None] * len(args)
        ends = out_blocks if out_blocks is not None else [None] * len(outs)
        out_specs = [spec(b, o) for b, o in zip(ends, outs)]
        return pl.pallas_call(
            kernel,
            out_shape=outs if len(outs) > 1 else outs[0],
            grid_spec=pltpu.PrefetchScalarGridSpec(
                num_scalar_prefetch=len(order),
                grid=(grid or 1,),
                in_specs=[spec(b, a) for b, a in zip(ins, args)],
                out_specs=out_specs if len(outs) > 1 else out_specs[0],
                scratch_shapes=scratch,
            ),
            compiler_params=pltpu.CompilerParams(vmem_limit_bytes=mib * 1024 * 1024),
            cost_estimate=pl.CostEstimate(flops=cost, bytes_accessed=1, transcendentals=0),
            name=name,
            input_output_aliases=aliases or {},
        )(*order, *args)

    return run


def shape(*dims, dtype=bf16):
    return jax.ShapeDtypeStruct(dims, dtype)


def exchange(packed, peers):
    out = lax.all_to_all(
        packed.reshape(peers, MAIN, packed.shape[1]), "expert", split_axis=0, concat_axis=0, tiled=True
    )
    return out.reshape(packed.shape)


class Ring:
    def __init__(self, name, size, inner, fast):
        self.name, self.size, self.inner, self.fast = name, size, inner, fast
        self.length = inner if fast else size // inner
        place = lax.axis_index(name)
        self.place = place % inner if fast else place // inner

    def step(self, i, k):
        outer, within = i // self.inner, i % self.inner
        if self.fast:
            return outer * self.inner + (within + k) % self.inner
        return (outer + k) % self.length * self.inner + within

    def send(self, array, k):
        if k % self.length == 0:
            return array
        return lax.ppermute(array, self.name, [(i, self.step(i, k)) for i in range(self.size)])

    def behind(self):
        steps = jnp.arange(self.length, dtype=jnp.int32)
        return ((self.place - steps) % self.length).astype(jnp.int32)

    def ahead(self):
        steps = jnp.arange(self.length, dtype=jnp.int32)
        return ((self.place + steps) % self.length).astype(jnp.int32)


def pair_sums(mine, theirs, y, name, wait=None, cost=1):
    count, depth, width = mine.shape
    steps = 2
    block = ((count, depth // steps, width), lambda i: (0, i, 0))
    flat = ((depth // steps, width), lambda i: (i, 0))
    kept, *sums = call(
        functools.partial(pair_kernel, count),
        name,
        shape(depth, width, dtype=f32),
        *[shape(depth, width)] * (count - 1),
        grid=steps,
        in_blocks=(block,) + (flat,) * count,
        out_blocks=(flat,) * count,
        cost=cost,
    )(mine, *theirs)
    return kept, [part if k == wait else y.send(part, -k - 1) for k, part in enumerate(sums)]


def total_sums(kept, parts):
    steps = 4
    flat = [((k.shape[0] // steps, k.shape[1]), lambda i: (i, 0)) for k in kept]
    count = len(parts[0])
    return call(
        total_kernel,
        "total",
        *[shape(*k.shape, dtype=f32) for k in kept],
        grid=steps,
        in_blocks=flat + [flat[0]] * count + [flat[1]] * count,
        out_blocks=flat,
    )(*kept, *parts[0], *parts[1])


def on_device(groups, frames, gain, router, w_in, w_out, expert_ids, frame_mask, out_grad):
    count, width = frames.shape
    peers = router.shape[1]
    rows = peers * CAP
    packed = shape(peers * MAIN, width + LANES)
    part = functools.partial
    gain = gain[None]
    router_rows = router.T
    ids = expert_ids.T
    core, y = Ring("dp", groups, NC, True), Ring("dp", groups, NC, False)
    behind = y.behind() * NC
    holders = jnp.concatenate([behind + core.place, behind + 1 - core.place])
    half = groups // 2

    sent, normed, place = call(
        part(dispatch_kernel, peers), "dispatch", packed, shape(count, width), shape(2, count, dtype=jnp.int32), cost=LONG
    )(frames, gain, ids)
    arrived = exchange(sent, peers)
    sent_grads, meta = call(
        part(grads_kernel, peers), "grads", packed, shape(count, 16, dtype=f32), cost=LONG
    )(normed, router_rows, ids, frame_mask[None], place, out_grad)
    pieces_in = [y.send(w_in[0], k) for k in range(half)]
    shard, _, pieces_in = lax.optimization_barrier((w_out[0], meta, pieces_in))
    pieces_in += [core.send(piece, 1) for piece in pieces_in]
    pieces_out = [y.send(shard, k) if k != 2 else None for k in range(half)]
    shard, _ = lax.optimization_barrier((shard, pieces_out[1]))
    pieces_out[2] = y.send(shard, 2)
    sent_grads, pieces_in, pieces_out[1], pieces_out[3] = lax.optimization_barrier(
        (sent_grads, pieces_in, pieces_out[1], pieces_out[3])
    )
    arrived_grads = exchange(sent_grads, peers)

    inner = w_in.shape[2]
    block = 512
    column = ((rows, block), lambda i, order: (0, i))
    incoming, hidden, derivative, turned = call(
        part(first_kernel, peers),
        "first",
        shape(rows, width),
        shape(rows, inner),
        shape(rows, inner, dtype=f32),
        shape(width, rows),
        grid=inner // block,
        in_blocks=(None,) + (((width // groups, block), lambda i, order: (0, i)),) * groups,
        out_blocks=(None, column, column, None),
        scratch=[pltpu.VMEM((width, block), bf16)],
        order=(holders,),
    )(arrived, *pieces_in)
    hidden, pieces_out[2] = lax.optimization_barrier((hidden, pieces_out[2]))
    pieces_out += [core.send(piece, 1) for piece in pieces_out]
    block = 256
    expert_packed, weights_out = call(
        part(second_kernel, peers),
        "second",
        packed,
        shape(inner, width),
        grid=width // block,
        in_blocks=(None,) + (((inner // groups, block), lambda i, order: (0, i)),) * groups,
        out_blocks=(None, ((inner, block), lambda i, order: (0, i))),
        scratch=[pltpu.VMEM((rows, width), bf16)],
        order=(holders,),
    )(hidden, *pieces_out)
    expert_packed, arrived_grads = lax.optimization_barrier((expert_packed, arrived_grads))
    returned = exchange(expert_packed, peers)

    block = NC * inner // groups
    column = ((rows, block), lambda i, order, *_: (0, order[i]))
    split = ((half, width // groups, block), lambda i, order, *_: (0, 0, order[i]))
    whole = ((1, inner // groups, width), lambda i, *_: (i, 0, 0))
    grad_incoming, *in_theirs, in_mine, packed_grads, gain_expert = call(
        part(backward_kernel, peers),
        "backward",
        shape(rows, width),
        *[shape(width // groups, inner)] * half,
        shape(half, width // groups, inner),
        shape(peers * MAIN, width + 2 * LANES),
        shape(1, width, dtype=f32),
        grid=half,
        in_blocks=(
            None,
            column,
            ((block, width), lambda i, order, *_: (order[i], 0)),
            None,
            None,
            None,
        )
        + (((width // groups, block), lambda i, order, *_: (0, order[i])),) * groups,
        out_blocks=(None,) + (((width // groups, block), lambda i, order, *_: (0, order[i])),) * half + (split, (packed.shape, lambda i, *_: (0, 0)), None),
        scratch=[pltpu.VMEM((rows, width), f32), pltpu.VMEM((width, block), bf16)],
        order=(y.behind(), holders),
    )(arrived_grads, derivative, weights_out, turned, incoming, gain, *pieces_in)
    in_kept, in_parts = pair_sums(in_mine, [core.send(part, 1) for part in in_theirs], y, "in_pair")
    returned, packed_grads, in_kept = lax.optimization_barrier((returned, packed_grads, in_kept))

    last = ((peers * MAIN, LANES), lambda i: (0, 1 + width // LANES))
    sent_back, grad_logits = call(
        part(route_kernel, peers),
        "route",
        shape(peers * MAIN, width + 2 * LANES),
        shape(count, peers, dtype=f32),
        in_blocks=(None,) * 7 + ("any",),
        out_blocks=(last, None),
        aliases={7: 0},
    )(returned, normed, out_grad, meta, router_rows, gain, gain_expert, packed_grads)
    returned, sent_back = lax.optimization_barrier((returned, sent_back))
    back = exchange(sent_back, peers)
    grad_incoming, _ = lax.optimization_barrier((grad_incoming, grad_logits))
    *out_theirs, out_mine = call(
        outer_kernel,
        "outer",
        *[shape(inner // groups, width)] * half,
        shape(half, inner // groups, width),
        grid=half,
        in_blocks=(None, column),
        out_blocks=(None,) * half + (whole,),
        order=(y.behind(), core.place[None].astype(jnp.int32)),
        cost=LONG,
    )(grad_incoming, hidden)
    arrived_out, in_parts = lax.optimization_barrier(([core.send(part, 1) for part in out_theirs], in_parts))
    out_kept, out_parts = pair_sums(out_mine, arrived_out, y, "out_pair", wait=1)
    mixed = call(part(mixed_kernel, peers), "mixed", shape(count, width))(returned, frames, meta)
    back, out_kept, mixed = lax.optimization_barrier((back, out_kept, mixed))
    sums = call(
        part(tally_kernel, peers), "tally", shape(groups, 8, width // 4, dtype=f32), in_blocks=(last,), mib=4
    )(back)
    sums, out_parts = lax.optimization_barrier((sums, out_parts))
    sums = lax.all_to_all(sums, "dp", 0, 0, tiled=True)
    grad_frames = call(part(finish_kernel, peers), "finish", shape(count, width))(
        back, frames, gain, out_grad, meta, grad_logits, router_rows
    )
    sums, grad_frames, out_parts[1] = lax.optimization_barrier((sums, grad_frames, out_parts[1]))
    out_parts[1] = y.send(out_parts[1], -2)
    router_mine, gain_gradient = call(
        sum_kernel, "sum", shape(peers, 8, width // 8, dtype=f32), shape(1, width, dtype=f32), mib=4
    )(sums)
    router_sums = lax.all_to_all(router_mine, "expert", 0, 0, tiled=True)
    totals = total_sums((out_kept, in_kept), (out_parts, in_parts))
    router_sums, (grad_w_out, grad_w_in) = lax.optimization_barrier((router_sums, totals))
    grad_router = router_sums.reshape(peers, width).T
    return (mixed, grad_frames, grad_w_in[None], grad_w_out[None], grad_router, gain_gradient[0])


def solution(mesh):
    return jax.shard_map(
        functools.partial(on_device, mesh.shape["dp"]),
        mesh=mesh,
        in_specs=(
            P(("dp", "expert"), None),
            P(),
            P(),
            P("expert", "dp", None),
            P("expert", "dp", None),
            P(("dp", "expert"), None),
            P(("dp", "expert")),
            P(("dp", "expert"), None),
        ),
        out_specs=(
            P(("dp", "expert"), None),
            P(("dp", "expert"), None),
            P("expert", "dp", None),
            P("expert", "dp", None),
            P(),
            P(),
        ),
        check_vma=False,
    )
```
